512 devices in a mesh: row: 32 (over x, y, core), col: 16 (over z).
Axes of the slice: x: 4, y: 4, z: 16, core: 2. Of those that a mesh axis runs over, the one named last changes fastest.
Arguments:
- spectra: bfloat16 [128, 2, 33, 4096], P('row', None, None, 'col'), may hold values from -64 to 64
- tilt_ranges: int32 [128, 2], P('row'), may hold values from 8 to 64
Outputs:
- correlation: float32 [128, 128, 729], P('row', 'col')
The draws below stay inside these ranges and needn't reach their ends.
All inputs are finite; a program needn't handle non-finite values.
Results may differ from the reference program's by a relative error of at most 0.0003.
Values may be sent and summed in bfloat16 or wider, within the bound.
A program may use at most 128 MiB of HBM per device.

```python
import math
import jax
import jax.numpy as jnp
from jax import lax

EDGE = 64
HALF = 33
PLANE = 4096
REACH = 4
WINDOW = 729
SUBTOMOS = 128


def draw_spectra(key, part):
    key = jax.random.fold_in(key, 11)
    keys = jax.random.split(key, 4)
    flat = jnp.arange(PLANE, dtype=jnp.int32)
    freq_x = flat // EDGE
    freq_y = flat % EDGE
    signed_x = jnp.where(freq_x < EDGE // 2, freq_x, freq_x - EDGE)
    signed_y = jnp.where(freq_y < EDGE // 2, freq_y, freq_y - EDGE)
    freq_z = jnp.arange(HALF, dtype=jnp.int32)
    radius = (signed_x * signed_x + signed_y * signed_y)[None, :] + (freq_z * freq_z)[:, None]
    envelope = 1.0 / (1.0 + radius.astype(jnp.float32) * (64.0 / (EDGE * EDGE)))
    offsets = jax.random.randint(keys[0], (SUBTOMOS, 3), -3, 4)
    phase = jnp.mod(freq_x[None, None, :] * offsets[:, 0, None, None] + freq_y[None, None, :] * offsets[:, 1, None, None] + freq_z[None, :, None] * offsets[:, 2, None, None], EDGE)
    angle = phase.astype(jnp.float32) * (2.0 * math.pi / EDGE)
    common = jnp.clip(jax.random.normal(keys[1], (2, HALF, PLANE), jnp.float32), -4.0, 4.0)
    noise = jnp.clip(jax.random.normal(keys[2], (SUBTOMOS, 2, HALF, PLANE), jnp.float32), -4.0, 4.0)
    scale = jnp.exp(jax.random.uniform(keys[3], (SUBTOMOS,), jnp.float32, 0.0, math.log(8.0)))
    cosine = jnp.cos(angle)
    sine = jnp.sin(angle)
    rot_real = common[0][None] * cosine + common[1][None] * sine
    rot_imag = common[1][None] * cosine - common[0][None] * sine
    real = (rot_real + 0.8 * noise[:, 0]) * envelope[None] * scale[:, None, None]
    imag = (rot_imag + 0.8 * noise[:, 1]) * envelope[None] * scale[:, None, None]
    return jnp.clip(jnp.stack([real, imag], 1), -64.0, 64.0).astype(jnp.bfloat16)


def plant(result, key, smallest, high):
    dims = result.shape
    index_at = [jax.random.randint(jax.random.fold_in(key, axis), (), 0, dims[axis]) for axis in range(len(dims))]
    result = result.at[tuple(index_at)].set(smallest)
    longest = dims.index(max(dims))
    index_at[longest] = (index_at[longest] + 1) % dims[longest]
    return result.at[tuple(index_at)].set(high)


def setup_inputs(seed: int = 0) -> dict:
    key_of = jax.random.split(jax.random.key(seed), 3)
    spectra = draw_spectra(jax.random.fold_in(key_of[2], 71), 0)
    tilt_ranges = plant(jax.random.randint(key_of[1], (SUBTOMOS, 2), 8, 65), jax.random.fold_in(key_of[1], 1), 8, 64).astype(jnp.int32)
    return dict(spectra=spectra, tilt_ranges=tilt_ranges)


full_turn = 2.0 * 3.141592653589793

def axis_tables(count):
    freqs = jnp.arange(count, dtype=jnp.int32)
    shifts_lag = jnp.arange(-REACH, REACH + 1, dtype=jnp.int32)
    phase = jnp.mod(freqs[:, None] * shifts_lag[None, :], EDGE)
    angle = phase.astype(jnp.float32) * (full_turn / EDGE)
    return (jnp.cos(angle), jnp.sin(angle))

def reference(spectra, tilt_ranges):
    highest = lax.Precision.HIGHEST
    freq_z = jnp.arange(HALF, dtype=jnp.int32)
    weights = jnp.where((freq_z == 0) | (freq_z == EDGE // 2), 1.0, 2.0).astype(jnp.float32)
    freq_x = jnp.arange(EDGE, dtype=jnp.int32)
    signed_x = jnp.where(freq_x < EDGE // 2, freq_x, freq_x - EDGE)
    slopes = jnp.where(signed_x[None, :] > 0, tilt_ranges[:, 0:1], tilt_ranges[:, 1:2])
    masks = (16 * freq_z[None, :, None] <= slopes[:, None, :] * jnp.abs(signed_x)[None, None, :]).astype(jnp.float32)
    real = spectra[:, 0].astype(jnp.float32).reshape(SUBTOMOS, HALF, EDGE, EDGE)
    imag = spectra[:, 1].astype(jnp.float32).reshape(SUBTOMOS, HALF, EDGE, EDGE)
    power = lax.optimization_barrier(jnp.sum(real * real + imag * imag, axis=3)) * weights[None, :, None]
    edge_cos, edge_sin = axis_tables(EDGE)
    depth_cos, depth_sin = axis_tables(HALF)

    def one_row(index):
        own_real = real[index]
        own_imag = imag[index]
        joint = masks[index][None] * masks * weights[None, :, None]
        prod_real = (own_real[None] * real + own_imag[None] * imag) * joint[..., None]
        prod_imag = (own_imag[None] * real - own_real[None] * imag) * joint[..., None]
        y_real = jnp.einsum('jzxy,yb->jzxb', prod_real, edge_cos, precision=highest) - jnp.einsum('jzxy,yb->jzxb', prod_imag, edge_sin, precision=highest)
        y_imag = jnp.einsum('jzxy,yb->jzxb', prod_real, edge_sin, precision=highest) + jnp.einsum('jzxy,yb->jzxb', prod_imag, edge_cos, precision=highest)
        x_real = jnp.einsum('jzxb,xa->jzab', y_real, edge_cos, precision=highest) - jnp.einsum('jzxb,xa->jzab', y_imag, edge_sin, precision=highest)
        x_imag = jnp.einsum('jzxb,xa->jzab', y_real, edge_sin, precision=highest) + jnp.einsum('jzxb,xa->jzab', y_imag, edge_cos, precision=highest)
        window = jnp.einsum('jzab,zl->jabl', x_real, depth_cos, precision=highest) - jnp.einsum('jzab,zl->jabl', x_imag, depth_sin, precision=highest)
        energy_own = jnp.einsum('zx,jzx->j', power[index] * masks[index], masks, precision=highest)
        energy_other = jnp.einsum('zx,jzx->j', masks[index], power * masks, precision=highest)
        return window.reshape(SUBTOMOS, WINDOW) / jnp.sqrt(energy_own * energy_other)[:, None]
    return lax.map(one_row, jnp.arange(SUBTOMOS, dtype=jnp.int32))
```

```python
import functools
import math

import jax
import jax.numpy as jnp
import ml_dtypes
import numpy as np
from jax import lax
from jax.experimental import pallas as pl
from jax.experimental.pallas import tpu as pltpu
from jax.sharding import PartitionSpec as P

EDGE = 64
HALF = 33
REACH = 4
LAGS = 9
WINDOW = 729
PADDED = 768
TILES = HALF + 2
PIECE = 40
NT = (((1,), (1,)), ((), ()))


def split_np(x):
    high = x.astype(ml_dtypes.bfloat16)
    low = (x - high.astype(np.float64)).astype(ml_dtypes.bfloat16)
    return high, low


def y_table():
    freq = np.arange(EDGE)
    out = np.zeros((LAGS, 8, 128), np.float32)
    for i in range(LAGS):
        if i <= REACH:
            t = np.cos(2 * np.pi * freq * i / EDGE)
        else:
            t = np.sin(2 * np.pi * freq * (i - REACH) / EDGE)
        out[i, :, :EDGE] = t
        out[i, :4, EDGE:] = t
        out[i, 4:, EDGE:] = -t
    return out


def x_table(cols):
    out = np.zeros((cols, LAGS, 32, 2, 8, 4, 4), np.float64)
    for col in range(cols):
        for k in range(4):
            for lx in range(-REACH, REACH + 1):
                angle = 2 * np.pi * ((col * 4 + k) * lx % EDGE) / EDGE
                for r in range(8):
                    for s in range(4):
                        out[col, lx + REACH, r * 4 + s, 0, r, k, s] = math.cos(angle)
                        out[col, lx + REACH, r * 4 + s, 1, r, k, s] = -math.sin(angle)
    out = out.reshape(cols, LAGS * 32, 256)
    high, low = split_np(out)
    return np.concatenate([high, low], 1)


def z_coefs():
    weight = [1.0 if k in (0, 32) else 2.0 for k in range(HALF)]
    cos = [[weight[k] * math.cos(2 * math.pi * k * l / EDGE) for k in range(HALF)] for l in range(REACH + 1)]
    sin = [[weight[k] * math.sin(2 * math.pi * k * l / EDGE) for k in range(HALF)] for l in range(REACH + 1)]
    return cos, sin


def signed(freq_x):
    return jnp.where(freq_x < EDGE // 2, freq_x, freq_x - EDGE)


def observed(freq_z, freq_x, up, down):
    q = signed(freq_x)
    return 16 * freq_z <= jnp.where(q > 0, up, down) * jnp.abs(q)


def prepare(col, spectra, tilts, message, power, pieces):
    lanes = lax.broadcasted_iota(jnp.int32, (HALF, 256), 1)
    freq_z = lax.broadcasted_iota(jnp.int32, (HALF, 256), 0)
    freq_x = col * 4 + lanes // EDGE
    weight = jnp.where((freq_z == 0) | (freq_z == EDGE // 2), 1.0, 2.0).astype(jnp.float32)
    power[...] = jnp.zeros_like(power)
    row = lax.broadcasted_iota(jnp.int32, (16, 256), 0)
    lane = lax.broadcasted_iota(jnp.int32, (16, 256), 1)
    total = jnp.zeros((16, 128), jnp.float32)
    for s in range(4):
        mask = observed(freq_z, freq_x, tilts[s, 0], tilts[s, 1])
        real = jnp.where(mask, spectra[s, 0].astype(jnp.float32), 0.0)
        imag = jnp.where(mask, spectra[s, 1].astype(jnp.float32), 0.0)
        square = (real * real + imag * imag) * weight
        for p in range(3):
            power[PIECE * p : PIECE * p + HALF, :] = square
        chosen = jnp.where((row // 4 == lane // EDGE) & (row % 4 == s), 1.0, 0.0)
        total = total + lax.dot_general(
            chosen, power[...], NT, precision=lax.Precision.HIGHEST, preferred_element_type=jnp.float32
        )
        for k in range(4):
            part = slice(k * EDGE, (k + 1) * EDGE)
            pieces[:, k * 4 + s, :] = jnp.concatenate([real[:, part], imag[:, part]], axis=1)
    message[:HALF] = pieces[...].astype(jnp.bfloat16)
    lane = lax.broadcasted_iota(jnp.int32, (16, 128), 1)
    row = lax.broadcasted_iota(jnp.int32, (16, 128), 0)
    high = total.astype(jnp.bfloat16).astype(jnp.float32)
    rest = total - high
    mid = rest.astype(jnp.bfloat16).astype(jnp.float32)
    low = rest - mid
    third = lane // PIECE
    message[HALF] = jnp.where(third == 0, high, jnp.where(third == 1, mid, low)).astype(jnp.bfloat16)
    s = row % 4
    up, down = (
        jnp.where(s == 0, tilts[0, i], jnp.where(s == 1, tilts[1, i], jnp.where(s == 2, tilts[2, i], tilts[3, i])))
        for i in range(2)
    )
    at = lane - third * PIECE
    mask = observed(at, col * 4 + row // 4, up, down) & (at < HALF) & (third < 3)
    message[HALF + 1] = jnp.where(mask, 1.0, 0.0).astype(jnp.bfloat16)


def modulate(block, table, mod):
    def one(z, carry):
        base = block[z].astype(jnp.float32)
        turned = pltpu.roll(base, EDGE, 1)
        highs, lows = [], []
        for k in range(4):
            both = jnp.concatenate([base[4 * k : 4 * k + 4], turned[4 * k : 4 * k + 4]], axis=0)
            for i in range(LAGS):
                value = both * table[i]
                high = value.astype(jnp.bfloat16)
                highs.append(high)
                lows.append((value - high.astype(jnp.float32)).astype(jnp.bfloat16))
        mod[z, :, :128] = jnp.concatenate(highs, axis=0)
        mod[z, :, 128:] = jnp.concatenate(lows, axis=0)
        return carry

    lax.fori_loop(0, HALF, one, 0, unroll=3)


def window_tile(own, mod, blocks, depth, quads):
    lane_k = (lax.broadcasted_iota(jnp.int32, (8, 128), 1) // 4) % 4

    def diagonal(values):
        lane = jnp.concatenate([lane_k] * (values[0].shape[0] // 8), axis=0) if values[0].shape[0] > 8 else lane_k
        out = values[3]
        for k in (2, 1, 0):
            out = jnp.where(lane == k, values[k], out)
        return out

    def one(z, carry):
        tile = blocks(z)
        product = lax.dot_general(
            mod[z], jnp.concatenate([tile, tile], axis=1), NT, preferred_element_type=jnp.float32
        )
        depth[z] = diagonal([product[72 * k : 72 * k + 72] for k in range(4)]).reshape(LAGS, 8, 128)
        return carry

    lax.fori_loop(0, HALF, one, 0, unroll=11)

    energies = []
    for own_tile, other in ((HALF, HALF + 1), (HALF + 1, HALF)):
        product = lax.dot_general(own[own_tile], blocks(other), NT, preferred_element_type=jnp.float32)
        picked = jnp.zeros((4, 128), jnp.float32)
        for k in range(4):
            picked = jnp.where(lane_k[:4] == k, product[4 * k : 4 * k + 4], picked)
        energies.append(jnp.concatenate([picked, jnp.zeros((4, 128), jnp.float32)], axis=0))

    cos, sin = z_coefs()

    def along_z(i, carry):
        value = [depth[z, i] for z in range(HALF)]
        even = [value[z] + value[32 - z] for z in range(16)] + [value[16]]
        odd = [value[z] - value[32 - z] for z in range(16)] + [value[16]]
        for lag in range(REACH + 1):
            source = even if lag % 2 == 0 else odd
            total = None
            for z in range(17):
                c = cos[lag][z]
                if z == 16 and lag % 2 == 1 or abs(c) < 1e-12:
                    continue
                term = source[z] * c
                total = term if total is None else total + term
            quads[lag, i] = total
        for lag in range(1, REACH + 1):
            source = odd if lag % 2 == 0 else even
            total = None
            for z in range(17):
                c = sin[lag][z]
                if z == 16 and lag % 2 == 0 or abs(c) < 1e-12:
                    continue
                term = source[z] * c
                total = term if total is None else total + term
            quads[REACH + lag, i] = total
        return carry

    lax.fori_loop(0, LAGS, along_z, 0)

    half = lax.broadcasted_iota(jnp.int32, (8, 128), 0) < 4

    def times_i(x):
        y = pltpu.roll(x, 4, 0)
        return jnp.where(half, -y, y)

    q = {}
    for ly in range(REACH + 1):
        for lz in range(REACH + 1):
            cc = quads[lz, ly]
            if ly == 0 and lz == 0:
                q[0, 0] = cc
            elif ly == 0:
                g = times_i(quads[REACH + lz, 0])
                q[0, lz], q[0, -lz] = cc + g, cc - g
            elif lz == 0:
                g = times_i(quads[0, REACH + ly])
                q[ly, 0], q[-ly, 0] = cc + g, cc - g
            else:
                ss = quads[REACH + lz, REACH + ly]
                sc = quads[lz, REACH + ly]
                cs = quads[REACH + lz, ly]
                p, m = cc - ss, cc + ss
                g, h = times_i(sc + cs), times_i(sc - cs)
                q[ly, lz], q[-ly, -lz] = p + g, p - g
                q[ly, -lz], q[-ly, lz] = m + h, m - h
    order = [q[ly, lz] for ly in range(-REACH, REACH + 1) for lz in range(-REACH, REACH + 1)] + energies
    order = order + [jnp.zeros((8, 128), jnp.float32)] * 5
    return order


def window_out(order_ref, xt, s):
    real = order_ref[pl.ds(s, 88, stride=8), :]
    imag = order_ref[pl.ds(4 + s, 88, stride=8), :]
    value = jnp.concatenate([real, imag], axis=1)
    high = value.astype(jnp.bfloat16)
    low = (value - high.astype(jnp.float32)).astype(jnp.bfloat16)
    x_high, x_low = xt[:288], xt[288:]
    dot = functools.partial(lax.dot_general, dimension_numbers=NT, preferred_element_type=jnp.float32)
    out = dot(x_high, high) + (dot(x_low, high) + dot(x_high, low))
    pieces = [out[32 * i : 32 * i + 32, :81] for i in range(LAGS)]
    energy = out[32 * REACH : 32 * REACH + 32, 81:83]
    fill = jnp.zeros((32, PADDED - WINDOW - 2), jnp.float32)
    return jnp.concatenate(pieces + [energy, fill], axis=1)


def flip_rows(rows):
    moved = pltpu.roll(rows, PADDED - WINDOW, 1)
    stacked = jnp.concatenate([moved[:, 128 * (5 - i) : 128 * (6 - i)] for i in range(6)], axis=0)
    row = lax.broadcasted_iota(jnp.int32, (128, 128), 0)
    lane = lax.broadcasted_iota(jnp.int32, (128, 128), 1)
    swap = jnp.where(row + lane == 127, 1.0, 0.0).astype(jnp.bfloat16)
    out = None
    for _ in range(3):
        high = stacked.astype(jnp.bfloat16)
        stacked = stacked - high.astype(jnp.float32)
        part = jnp.dot(high, swap, preferred_element_type=jnp.float32)
        out = part if out is None else out + part
    return out


def fused_kernel(
    spectra_any, tilts_any, table_any, tables_any, out,
    spectra, tilts, table, xt, power, pieces, own, mods, lanes, mod, depth, quads, order,
    part, extra, from_left, from_right, extra_in, sent, final, turned,
    local_sem, x_send, x_recv, y_send, y_recv, right_send, right_recv, left_send, left_recv,
    extra_send, extra_recv, final_send, final_recv,
):
    row = lax.axis_index("row")
    z = lax.axis_index("col")
    xx, yy, core = row // 8, (row // 2) % 4, row % 2
    zx, zy = z // 4, z % 4
    chip = xx * 4 + yy

    def at(x, y, c, depth_z):
        return {"row": (x * 4 + y) * 2 + c, "col": depth_z}

    locals_ = [
        pltpu.make_async_copy(spectra_any, spectra, local_sem.at[0]),
        pltpu.make_async_copy(tilts_any, tilts, local_sem.at[1]),
        pltpu.make_async_copy(table_any, table, local_sem.at[2]),
        pltpu.make_async_copy(tables_any.at[z], xt, local_sem.at[3]),
    ]
    for copy in locals_:
        copy.start()

    barrier = pltpu.get_barrier_semaphore()

    def greet(target):
        pl.semaphore_signal(barrier, inc=1, device_id=target, device_id_type=pl.DeviceIdType.MESH)

    for i in range(1, 4):
        greet(at(lax.rem(xx + i, 4), yy, core, z))
        greet(at(xx, lax.rem(yy + i, 4), 0, z))
        greet(at(xx, lax.rem(yy + i, 4), 1, z))
    greet(at(xx, yy, 1 - core, z))
    right, left = lax.rem(z + 1, 16), lax.rem(z + 15, 16)
    greet(at(xx, yy, core, right))
    greet(at(xx, yy, core, left))

    @pl.when(zx != xx)
    def _():
        greet(at(zx, yy, core, xx * 4 + zy))

    @pl.when(zy != yy)
    def _():
        greet(at(xx, zy, 0, zx * 4 + yy))
        greet(at(xx, zy, 1, zx * 4 + yy))

    locals_[0].wait()
    locals_[1].wait()
    prepare(z, spectra, tilts, own, power, pieces)
    count = 12 + jnp.where(zx != xx, 1, 0) + jnp.where(zy != yy, 2, 0)
    pl.semaphore_wait(barrier, count)

    def remote(src, dst, send, recv, target):
        return pltpu.make_async_remote_copy(
            src_ref=src, dst_ref=dst, send_sem=send, recv_sem=recv,
            device_id=target, device_id_type=pl.DeviceIdType.MESH,
        )

    gathers = []
    for i in range(1, 4):
        y = lax.rem(yy + i, 4)
        there = jnp.where(y < yy, core, 1 - core)
        gathers.append(remote(own, lanes.at[yy], y_send.at[i], y_recv.at[yy], at(xx, y, there, z)))
    gathers.append(remote(own, lanes.at[4], y_send.at[0], y_recv.at[4], at(xx, yy, 1 - core, z)))
    for i in range(1, 4):
        x = lax.rem(xx + i, 4)
        gathers.append(remote(own, mods.at[xx], x_send.at[i], x_recv.at[xx], at(x, yy, core, z)))
    for copy in gathers:
        copy.start()

    lanes[yy] = own[...]
    mods[xx] = own[...]
    lanes[5:8] = jnp.zeros((3, TILES, 16, 128), jnp.bfloat16)
    locals_[2].wait()
    modulate(own, table, mod.at[0])
    locals_[3].wait()

    def wait_lane(slot):
        remote(own, lanes.at[slot], y_send.at[0], y_recv.at[slot], at(xx, yy, 1 - core, z)).wait_recv()

    for i in range(1, 4):
        wait_lane(lax.rem(yy + i, 4))
    wait_lane(4)

    def move_right(step):
        chunk = lax.rem(z + 9 - step, 16)
        if step > 1:
            before = remote(part.at[chunk], from_left.at[step - 2], right_send.at[step - 2], right_recv.at[step - 2], at(xx, yy, core, right))
            before.wait_recv()
            part[chunk] = part[chunk] + from_left[step - 2]
        remote(part.at[chunk], from_left.at[step - 1], right_send.at[step - 1], right_recv.at[step - 1], at(xx, yy, core, right)).start()

        @pl.when(chunk == chip)
        def _():
            copy = remote(extra, extra_in.at[0], extra_send.at[0], extra_recv.at[0], at(xx, yy, core, right))
            if step > 1:
                copy.wait_recv()
                extra[...] = extra[...] + extra_in[0]
            copy.start()

    def move_left(step):
        chunk = lax.rem(z + 8 + step, 16)
        if step > 1:
            before = remote(part.at[chunk], from_right.at[step - 2], left_send.at[step - 2], left_recv.at[step - 2], at(xx, yy, core, left))
            before.wait_recv()
            part[chunk] = part[chunk] + from_right[step - 2]
        remote(part.at[chunk], from_right.at[step - 1], left_send.at[step - 1], left_recv.at[step - 1], at(xx, yy, core, left)).start()

        @pl.when(chunk == chip)
        def _():
            copy = remote(extra, extra_in.at[1], extra_send.at[0], extra_recv.at[1], at(xx, yy, core, left))
            if step > 1:
                copy.wait_recv()
                extra[...] = extra[...] + extra_in[1]
            copy.start()

    second = jnp.where(zy < 2, 1, 3)

    def task(q, carry):
        turn = jnp.where(q == 0, 2, jnp.where(q == 1, second, jnp.where(q == 2, 4 - second, 0)))
        x = lax.rem(zx + turn, 4)

        @pl.when(x != xx)
        def _():
            remote(own, mods.at[x], x_send.at[0], x_recv.at[x], at(xx, yy, 1 - core, z)).wait_recv()
            modulate(mods.at[x], table, mod.at[1])

        def blocks(k):
            return lanes[:, k].reshape(128, 128)

        rows = window_tile(mods.at[x], mod.at[jnp.where(x == xx, 0, 1)], blocks, depth, quads)
        order[...] = jnp.concatenate(rows, axis=0)
        for s in range(4):
            value = window_out(order, xt, s)
            other = value[16:20]
            for y in range(4):
                swap = (yy == y) & (x < xx)
                part[x * 4 + y, 4 * s : 4 * s + 4, :] = jnp.where(swap, other, value[4 * y : 4 * y + 4])

            @pl.when(x == xx)
            def _():
                extra[4 * s : 4 * s + 4, :] = other

        @pl.when(q == 0)
        def _():
            move_right(1)

        @pl.when(q == 1)
        def _():
            for step in (2, 3):
                move_right(step)
                move_left(step - 1)

        @pl.when(q == 2)
        def _():
            for step in (4, 5):
                move_right(step)
                move_left(step - 1)

        return carry

    lax.fori_loop(0, 4, task, 0)
    for step in (6, 7, 8):
        move_right(step)
        move_left(step - 1)
    remote(part.at[z], from_left.at[7], right_send.at[7], right_recv.at[7], at(xx, yy, core, right)).wait_recv()
    remote(part.at[z], from_right.at[6], left_send.at[6], left_recv.at[6], at(xx, yy, core, left)).wait_recv()

    def scaled(total):
        return total / jnp.sqrt(total[:, WINDOW : WINDOW + 1] * total[:, WINDOW + 1 : WINDOW + 2])

    value = scaled(part[z] + from_left[7] + from_right[6])
    same_x = zx == xx
    home = z == chip
    keep = (zy == yy) & (zx >= xx)
    to_direct = remote(sent.at[0], final.at[0], final_send.at[0], final_recv.at[0], at(zx, yy, core, xx * 4 + zy))
    partner = jnp.where(zy != yy, jnp.where(yy < zy, core, 1 - core), 1 - core)
    to_turned = remote(sent.at[1], final.at[1], final_send.at[1], final_recv.at[1], at(xx, zy, partner, zx * 4 + yy))

    @pl.when(same_x)
    def _():
        final[0] = value

    @pl.when(jnp.logical_not(same_x))
    def _():
        sent[0] = value
        to_direct.start()

    turned[...] = flip_rows(value)
    flipped = jnp.concatenate(
        [
            jnp.concatenate([turned[pl.ds(16 * i + s, 4, stride=4), :] for i in range(6)], axis=1)
            for s in range(4)
        ],
        axis=0,
    )

    @pl.when(keep & jnp.logical_not(home))
    def _():
        final[1] = flipped

    @pl.when(jnp.logical_not(keep))
    def _():
        sent[1] = flipped
        to_turned.start()

    @pl.when(home)
    def _():
        for i, send in ((0, right), (1, left)):
            remote(extra, extra_in.at[i], extra_send.at[0], extra_recv.at[i], at(xx, yy, core, send)).wait_recv()
        final[1] = scaled(extra[...] + extra_in[0] + extra_in[1])

    @pl.when(jnp.logical_not(same_x))
    def _():
        to_direct.wait_recv()

    @pl.when(jnp.logical_not(keep))
    def _():
        to_turned.wait_recv()

    first = jnp.where(
        zy != yy,
        jnp.where(yy < zy, core, 1 - core),
        jnp.where(zx <= xx, core, 1 - core),
    )
    one, two = final[0], final[1]
    low = jnp.where(first == 0, one, two)
    high = jnp.where(first == 0, two, one)
    for a in range(4):
        out[a] = jnp.concatenate([low[4 * a : 4 * a + 4, :WINDOW], high[4 * a : 4 * a + 4, :WINDOW]], axis=0)

    @pl.when(jnp.logical_not(same_x))
    def _():
        to_direct.wait_send()

    @pl.when(jnp.logical_not(keep))
    def _():
        to_turned.wait_send()

    for copy in gathers:
        copy.wait_send()
    for i in range(8):
        remote(part.at[i], from_left.at[i], right_send.at[i], right_recv.at[i], at(xx, yy, core, right)).wait_send()
    for i in range(7):
        remote(part.at[i], from_right.at[i], left_send.at[i], left_recv.at[i], at(xx, yy, core, left)).wait_send()

    @pl.when(jnp.logical_not(home))
    def _():
        remote(extra, extra_in.at[0], extra_send.at[0], extra_recv.at[0], at(xx, yy, core, right)).wait_send()


def body(x_tables, table, spectra, tilt_ranges):
    anywhere = pl.BlockSpec(memory_space=pl.ANY)
    f32, bf16 = jnp.float32, jnp.bfloat16
    dma = pltpu.SemaphoreType.DMA
    return pl.pallas_call(
        fused_kernel,
        out_shape=jax.ShapeDtypeStruct((4, 8, WINDOW), f32),
        in_specs=[anywhere] * 4,
        out_specs=pl.BlockSpec(memory_space=pltpu.VMEM),
        scratch_shapes=[
            pltpu.VMEM((4, 2, HALF, 256), bf16),
            pltpu.SMEM((4, 2), jnp.int32),
            pltpu.VMEM((LAGS, 8, 128), f32),
            pltpu.VMEM((576, 256), bf16),
            pltpu.VMEM((128, 256), f32),
            pltpu.VMEM((HALF, 16, 128), f32),
            pltpu.VMEM((TILES, 16, 128), bf16),
            pltpu.VMEM((4, TILES, 16, 128), bf16),
            pltpu.VMEM((8, TILES, 16, 128), bf16),
            pltpu.VMEM((2, HALF, 288, 256), bf16),
            pltpu.VMEM((HALF, LAGS, 8, 128), f32),
            pltpu.VMEM((LAGS, LAGS, 8, 128), f32),
            pltpu.VMEM((88 * 8, 128), f32),
            pltpu.VMEM((16, 16, PADDED), f32),
            pltpu.VMEM((16, PADDED), f32),
            pltpu.VMEM((8, 16, PADDED), f32),
            pltpu.VMEM((7, 16, PADDED), f32),
            pltpu.VMEM((2, 16, PADDED), f32),
            pltpu.VMEM((2, 16, PADDED), f32),
            pltpu.VMEM((2, 16, PADDED), f32),
            pltpu.VMEM((96, 128), f32),
            dma((4,)),
            dma((4,)),
            dma((4,)),
            dma((4,)),
            dma((5,)),
            dma((8,)),
            dma((8,)),
            dma((7,)),
            dma((7,)),
            dma((1,)),
            dma((2,)),
            dma((2,)),
            dma((2,)),
        ],
        compiler_params=pltpu.CompilerParams(
            vmem_limit_bytes=48 * 1024 * 1024, collective_id=0, has_side_effects=True
        ),
    )(spectra, tilt_ranges, table, x_tables)


def solution(mesh):
    cols = mesh.shape["col"]
    inner = functools.partial(body, jnp.asarray(x_table(cols)), jnp.asarray(y_table()))
    return jax.shard_map(
        inner,
        mesh=mesh,
        in_specs=(P("row", None, None, "col"), P("row", None)),
        out_specs=P("row", "col", None),
        check_vma=False,
    )
```

```python
import functools
import math

import jax
import jax.numpy as jnp
import ml_dtypes
import numpy as np
from jax import lax
from jax.experimental import pallas as pl
from jax.experimental.pallas import tpu as pltpu
from jax.sharding import PartitionSpec as P

EDGE = 64
HALF = 33
REACH = 4
LAGS = 9
WINDOW = 729
PADDED = 768
TILES = HALF + 2
PIECE = 40
ROWS = 24
NT = (((1,), (1,)), ((), ()))


def split_np(x):
    high = x.astype(ml_dtypes.bfloat16)
    low = (x - high.astype(np.float64)).astype(ml_dtypes.bfloat16)
    return high, low


def y_table():
    freq = np.arange(EDGE)
    out = np.zeros((LAGS, 8, 128), np.float32)
    for i in range(LAGS):
        if i <= REACH:
            t = np.cos(2 * np.pi * freq * i / EDGE)
        else:
            t = np.sin(2 * np.pi * freq * (i - REACH) / EDGE)
        out[i, :, :EDGE] = t
        out[i, :4, EDGE:] = t
        out[i, 4:, EDGE:] = -t
    return out


def x_table(cols):
    out = np.zeros((cols, LAGS, ROWS, 2, 8, 4, 4), np.float64)
    for col in range(cols):
        for k in range(4):
            for lx in range(-REACH, REACH + 1):
                angle = 2 * np.pi * ((col * 4 + k) * lx % EDGE) / EDGE
                for r in range(ROWS // 4):
                    for s in range(4):
                        out[col, lx + REACH, r * 4 + s, 0, r, k, s] = math.cos(angle)
                        out[col, lx + REACH, r * 4 + s, 1, r, k, s] = -math.sin(angle)
    out = out.reshape(cols, LAGS * ROWS, 256)
    out = np.pad(out, ((0, 0), (0, 224 - LAGS * ROWS), (0, 0)))
    return np.stack(split_np(out), 1)


def z_coefs():
    weight = [1.0 if k in (0, 32) else 2.0 for k in range(HALF)]
    cos = [[weight[k] * math.cos(2 * math.pi * k * l / EDGE) for k in range(HALF)] for l in range(REACH + 1)]
    sin = [[weight[k] * math.sin(2 * math.pi * k * l / EDGE) for k in range(HALF)] for l in range(REACH + 1)]
    return cos, sin


def signed(freq_x):
    return jnp.where(freq_x < EDGE // 2, freq_x, freq_x - EDGE)


def observed(freq_z, freq_x, up, down):
    q = signed(freq_x)
    return 16 * freq_z <= jnp.where(q > 0, up, down) * jnp.abs(q)


def prepare(col, spectra, tilts, message, power, pieces):
    lanes = lax.broadcasted_iota(jnp.int32, (HALF, 256), 1)
    freq_z = lax.broadcasted_iota(jnp.int32, (HALF, 256), 0)
    freq_x = col * 4 + lanes // EDGE
    weight = jnp.where((freq_z == 0) | (freq_z == EDGE // 2), 1.0, 2.0).astype(jnp.float32)
    power[...] = jnp.zeros_like(power)
    row = lax.broadcasted_iota(jnp.int32, (16, 256), 0)
    lane = lax.broadcasted_iota(jnp.int32, (16, 256), 1)
    total = jnp.zeros((16, 128), jnp.float32)
    for s in range(4):
        mask = observed(freq_z, freq_x, tilts[s, 0], tilts[s, 1])
        real = jnp.where(mask, spectra[s, 0].astype(jnp.float32), 0.0)
        imag = jnp.where(mask, spectra[s, 1].astype(jnp.float32), 0.0)
        square = (real * real + imag * imag) * weight
        for p in range(3):
            power[PIECE * p : PIECE * p + HALF, :] = square
        chosen = jnp.where((row // 4 == lane // EDGE) & (row % 4 == s), 1.0, 0.0)
        total = total + lax.dot_general(
            chosen, power[...], NT, precision=lax.Precision.HIGHEST, preferred_element_type=jnp.float32
        )
        for k in range(4):
            part = slice(k * EDGE, (k + 1) * EDGE)
            pieces[:, k * 4 + s, :] = jnp.concatenate([real[:, part], imag[:, part]], axis=1)
    message[:HALF] = pieces[...].astype(jnp.bfloat16)
    lane = lax.broadcasted_iota(jnp.int32, (16, 128), 1)
    row = lax.broadcasted_iota(jnp.int32, (16, 128), 0)
    high = total.astype(jnp.bfloat16).astype(jnp.float32)
    rest = total - high
    mid = rest.astype(jnp.bfloat16).astype(jnp.float32)
    low = rest - mid
    third = lane // PIECE
    message[HALF] = jnp.where(third == 0, high, jnp.where(third == 1, mid, low)).astype(jnp.bfloat16)
    s = row % 4
    up, down = (
        jnp.where(s == 0, tilts[0, i], jnp.where(s == 1, tilts[1, i], jnp.where(s == 2, tilts[2, i], tilts[3, i])))
        for i in range(2)
    )
    at = lane - third * PIECE
    mask = observed(at, col * 4 + row // 4, up, down) & (at < HALF) & (third < 3)
    message[HALF + 1] = jnp.where(mask, 1.0, 0.0).astype(jnp.bfloat16)


def modulate(block, table, mod):
    def one(z, carry):
        base = block[z].astype(jnp.float32)
        turned = pltpu.roll(base, EDGE, 1)
        values = []
        for k in range(0, 4, 2):
            a, b = base[4 * k : 4 * k + 8], turned[4 * k : 4 * k + 8]
            for both in (
                jnp.where(first, a, pltpu.roll(b, 4, 0)),
                jnp.where(first, pltpu.roll(a, 4, 0), b),
            ):
                values += [both * table[i] for i in range(LAGS)]
        value = jnp.concatenate(values, axis=0)
        high = value.astype(jnp.bfloat16)
        mod[z, :, :128] = high
        mod[z, :, 128:] = (value - high.astype(jnp.float32)).astype(jnp.bfloat16)
        return carry

    first = lax.broadcasted_iota(jnp.int32, (8, 128), 0) < 4

    lax.fori_loop(0, HALF, one, 0, unroll=11)


def window_tile(own, mod, blocks, depth, quads, middle):
    lane_k = (lax.broadcasted_iota(jnp.int32, (8, 128), 1) // 4) % 4

    def diagonal(values):
        lane = jnp.concatenate([lane_k] * (values[0].shape[0] // 8), axis=0) if values[0].shape[0] > 8 else lane_k
        out = values[3]
        for k in (2, 1, 0):
            out = jnp.where(lane == k, values[k], out)
        return out

    def one(z, carry):
        tile = blocks(z)
        product = lax.dot_general(
            mod[z], jnp.concatenate([tile, tile], axis=1), NT, preferred_element_type=jnp.float32
        )
        depth[z] = diagonal([product[72 * k : 72 * k + 72] for k in range(4)]).reshape(LAGS, 8, 128)
        return carry

    lax.fori_loop(0, HALF, one, 0, unroll=11)

    middle()
    energies = []
    for own_tile, other in ((HALF, HALF + 1), (HALF + 1, HALF)):
        product = lax.dot_general(own[own_tile], blocks(other), NT, preferred_element_type=jnp.float32)
        picked = jnp.zeros((4, 128), jnp.float32)
        for k in range(4):
            picked = jnp.where(lane_k[:4] == k, product[4 * k : 4 * k + 4], picked)
        energies.append(jnp.concatenate([picked, jnp.zeros((4, 128), jnp.float32)], axis=0))

    cos, sin = z_coefs()

    def along_z(i, carry):
        value = [depth[z, i] for z in range(HALF)]
        even = [value[z] + value[32 - z] for z in range(16)] + [value[16]]
        odd = [value[z] - value[32 - z] for z in range(16)] + [value[16]]
        for lag in range(REACH + 1):
            source = even if lag % 2 == 0 else odd
            total = None
            for z in range(17):
                c = cos[lag][z]
                if z == 16 and lag % 2 == 1 or abs(c) < 1e-12:
                    continue
                term = source[z] * c
                total = term if total is None else total + term
            quads[lag, i] = total
        for lag in range(1, REACH + 1):
            source = odd if lag % 2 == 0 else even
            total = None
            for z in range(17):
                c = sin[lag][z]
                if z == 16 and lag % 2 == 0 or abs(c) < 1e-12:
                    continue
                term = source[z] * c
                total = term if total is None else total + term
            quads[REACH + lag, i] = total
        return carry

    lax.fori_loop(0, LAGS, along_z, 0)

    half = lax.broadcasted_iota(jnp.int32, (8, 128), 0) < 4

    def times_i(x):
        y = pltpu.roll(x, 4, 0)
        return jnp.where(half, -y, y)

    q = {}
    for ly in range(REACH + 1):
        for lz in range(REACH + 1):
            cc = quads[lz, ly]
            if ly == 0 and lz == 0:
                q[0, 0] = cc
            elif ly == 0:
                g = times_i(quads[REACH + lz, 0])
                q[0, lz], q[0, -lz] = cc + g, cc - g
            elif lz == 0:
                g = times_i(quads[0, REACH + ly])
                q[ly, 0], q[-ly, 0] = cc + g, cc - g
            else:
                ss = quads[REACH + lz, REACH + ly]
                sc = quads[lz, REACH + ly]
                cs = quads[REACH + lz, ly]
                p, m = cc - ss, cc + ss
                g, h = times_i(sc + cs), times_i(sc - cs)
                q[ly, lz], q[-ly, -lz] = p + g, p - g
                q[ly, -lz], q[-ly, lz] = m + h, m - h
    order = [q[ly, lz] for ly in range(-REACH, REACH + 1) for lz in range(-REACH, REACH + 1)] + energies
    order = order + [jnp.zeros((8, 128), jnp.float32)] * 5
    return order


def window_out(order_ref, xt, s):
    real = order_ref[pl.ds(s, 88, stride=8), :]
    imag = order_ref[pl.ds(4 + s, 88, stride=8), :]
    value = jnp.concatenate([real, imag], axis=1)
    high = value.astype(jnp.bfloat16)
    low = (value - high.astype(jnp.float32)).astype(jnp.bfloat16)
    x_high, x_low = xt[0], xt[1]
    dot = functools.partial(lax.dot_general, dimension_numbers=NT, preferred_element_type=jnp.float32)
    out = dot(x_high, high) + (dot(x_low, high) + dot(x_high, low))
    pieces = [out[ROWS * i : ROWS * i + ROWS, :81] for i in range(LAGS)]
    energy = out[ROWS * REACH : ROWS * REACH + ROWS, 81:83]
    fill = jnp.zeros((ROWS, PADDED - WINDOW - 2), jnp.float32)
    return jnp.concatenate(pieces + [energy, fill], axis=1)


def write_part(x, xx, yy, order, xt, part):
    first = lax.broadcasted_iota(jnp.int32, (8, PADDED), 0) < 4
    for pair in range(2):
        a, b = window_out(order, xt, 2 * pair), window_out(order, xt, 2 * pair + 1)
        blocks = []
        for i in range(0, ROWS, 8):
            upper, lower = a[i : i + 8], b[i : i + 8]
            blocks.append(jnp.where(first, upper, pltpu.roll(lower, 4, 0)))
            blocks.append(jnp.where(first, pltpu.roll(upper, 4, 0), lower))
        for y in range(4):
            swap = (yy == y) & (x < xx)
            part[x * 4 + y, 8 * pair : 8 * pair + 8, :] = jnp.where(swap, blocks[4], blocks[y])

        @pl.when(x == xx)
        def _():
            part[16, 8 * pair : 8 * pair + 8, :] = blocks[4]


def flip_rows(rows):
    moved = pltpu.roll(rows, PADDED - WINDOW, 1)
    stacked = jnp.concatenate([moved[:, 128 * (5 - i) : 128 * (6 - i)] for i in range(6)], axis=0)
    row = lax.broadcasted_iota(jnp.int32, (128, 128), 0)
    lane = lax.broadcasted_iota(jnp.int32, (128, 128), 1)
    swap = jnp.where(row + lane == 127, 1.0, 0.0).astype(jnp.bfloat16)
    out = None
    for _ in range(3):
        high = stacked.astype(jnp.bfloat16)
        stacked = stacked - high.astype(jnp.float32)
        part = jnp.dot(high, swap, preferred_element_type=jnp.float32)
        out = part if out is None else out + part
    return out


def fused_kernel(
    spectra_any, tilts_any, table_any, tables_any, out,
    spectra, tilts, table, xt, power, pieces, own, mods, lanes, mod, depth, quads, order,
    part, from_left, from_right, extra_in, sent, final, turned,
    local_sem, x_send, x_recv, y_send, y_recv, right_send, right_recv, left_send, left_recv,
    extra_send, extra_recv, final_send, final_recv,
):
    row = lax.axis_index("row")
    z = lax.axis_index("col")
    xx, yy, core = row // 8, (row // 2) % 4, row % 2
    zx, zy = z // 4, z % 4
    chip = xx * 4 + yy

    def at(x, y, c, depth_z):
        return {"row": (x * 4 + y) * 2 + c, "col": depth_z}

    locals_ = [
        pltpu.make_async_copy(spectra_any, spectra, local_sem.at[0]),
        pltpu.make_async_copy(tilts_any, tilts, local_sem.at[1]),
        pltpu.make_async_copy(table_any, table, local_sem.at[2]),
        pltpu.make_async_copy(tables_any.at[z], xt, local_sem.at[3]),
    ]
    for copy in locals_:
        copy.start()

    barrier = pltpu.get_barrier_semaphore()

    def greet(target):
        pl.semaphore_signal(barrier, inc=1, device_id=target, device_id_type=pl.DeviceIdType.MESH)

    for i in range(1, 4):
        greet(at(lax.rem(xx + i, 4), yy, core, z))
        greet(at(xx, lax.rem(yy + i, 4), 0, z))
        greet(at(xx, lax.rem(yy + i, 4), 1, z))
    greet(at(xx, yy, 1 - core, z))
    right, left = lax.rem(z + 1, 16), lax.rem(z + 15, 16)
    greet(at(xx, yy, core, right))
    greet(at(xx, yy, core, left))

    @pl.when(zx != xx)
    def _():
        greet(at(zx, yy, core, xx * 4 + zy))

    @pl.when(zy != yy)
    def _():
        greet(at(xx, zy, 0, zx * 4 + yy))
        greet(at(xx, zy, 1, zx * 4 + yy))

    locals_[0].wait()
    locals_[1].wait()
    prepare(z, spectra, tilts, own, power, pieces)
    count = 12 + jnp.where(zx != xx, 1, 0) + jnp.where(zy != yy, 2, 0)
    pl.semaphore_wait(barrier, count)

    def remote(src, dst, send, recv, target):
        return pltpu.make_async_remote_copy(
            src_ref=src, dst_ref=dst, send_sem=send, recv_sem=recv,
            device_id=target, device_id_type=pl.DeviceIdType.MESH,
        )

    gathers = []
    for i in (1, 3, 2):
        y = lax.rem(yy + i, 4)
        there = jnp.where(y < yy, core, 1 - core)
        gathers.append(remote(own, lanes.at[yy], y_send.at[i], y_recv.at[yy], at(xx, y, there, z)))
        x = lax.rem(xx + i, 4)
        gathers.append(remote(own, mods.at[xx], x_send.at[i], x_recv.at[xx], at(x, yy, core, z)))
    gathers.append(remote(own, lanes.at[4], y_send.at[0], y_recv.at[4], at(xx, yy, 1 - core, z)))
    for copy in gathers:
        copy.start()

    lanes[yy] = own[...]
    mods[xx] = own[...]
    lanes[5:8] = jnp.zeros((3, TILES, 16, 128), jnp.bfloat16)
    locals_[2].wait()
    modulate(own, table, mod.at[0])
    locals_[3].wait()

    def wait_lane(slot):
        remote(own, lanes.at[slot], y_send.at[0], y_recv.at[slot], at(xx, yy, 1 - core, z)).wait_recv()

    for i in range(1, 4):
        wait_lane(lax.rem(yy + i, 4))
    wait_lane(4)

    def move_right(step):
        chunk = lax.rem(z + 9 - step, 16)
        if step > 1:
            before = remote(part.at[chunk], from_left.at[step - 2], right_send.at[step - 2], right_recv.at[step - 2], at(xx, yy, core, right))
            before.wait_recv()
            part[chunk] = part[chunk] + from_left[step - 2]
        remote(part.at[chunk], from_left.at[step - 1], right_send.at[step - 1], right_recv.at[step - 1], at(xx, yy, core, right)).start()

        @pl.when(chunk == chip)
        def _():
            copy = remote(part.at[16], extra_in.at[0], extra_send.at[0], extra_recv.at[0], at(xx, yy, core, right))
            if step > 1:
                copy.wait_recv()
                part[16] = part[16] + extra_in[0]
            copy.start()

    def move_left(step):
        chunk = lax.rem(z + 8 + step, 16)
        if step > 1:
            before = remote(part.at[chunk], from_right.at[step - 2], left_send.at[step - 2], left_recv.at[step - 2], at(xx, yy, core, left))
            before.wait_recv()
            part[chunk] = part[chunk] + from_right[step - 2]
        remote(part.at[chunk], from_right.at[step - 1], left_send.at[step - 1], left_recv.at[step - 1], at(xx, yy, core, left)).start()

        @pl.when(chunk == chip)
        def _():
            copy = remote(part.at[16], extra_in.at[1], extra_send.at[0], extra_recv.at[1], at(xx, yy, core, left))
            if step > 1:
                copy.wait_recv()
                part[16] = part[16] + extra_in[1]
            copy.start()

    second = jnp.where(zy < 2, 1, 3)

    def task(q, carry):
        turn = jnp.where(q == 0, 2, jnp.where(q == 1, second, jnp.where(q == 2, 4 - second, 0)))
        x = lax.rem(zx + turn, 4)

        @pl.when(x != xx)
        def _():
            remote(own, mods.at[x], x_send.at[0], x_recv.at[x], at(xx, yy, 1 - core, z)).wait_recv()
            modulate(mods.at[x], table, mod.at[1])

        def middle():
            for at_q, step in ((2, 3), (3, 5)):
                @pl.when(q == at_q)
                def _():
                    move_right(step)
                    move_left(step - 1)

        def blocks(k):
            return lanes[:, k].reshape(128, 128)

        rows = window_tile(mods.at[x], mod.at[jnp.where(x == xx, 0, 1)], blocks, depth, quads, middle)
        order[...] = jnp.concatenate(rows, axis=0)
        write_part(x, xx, yy, order, xt, part)

        @pl.when(q == 0)
        def _():
            move_right(1)

        @pl.when(q == 1)
        def _():
            move_right(2)
            move_left(1)

        @pl.when(q == 2)
        def _():
            move_right(4)
            move_left(3)

        return carry

    lax.fori_loop(0, 4, task, 0)
    for step in (6, 7, 8):
        move_right(step)
        move_left(step - 1)
    remote(part.at[z], from_left.at[7], right_send.at[7], right_recv.at[7], at(xx, yy, core, right)).wait_recv()
    remote(part.at[z], from_right.at[6], left_send.at[6], left_recv.at[6], at(xx, yy, core, left)).wait_recv()

    def scaled(total):
        return total / jnp.sqrt(total[:, WINDOW : WINDOW + 1] * total[:, WINDOW + 1 : WINDOW + 2])

    value = scaled(part[z] + from_left[7] + from_right[6])
    same_x = zx == xx
    home = z == chip
    keep = (zy == yy) & (zx >= xx)
    to_direct = remote(sent.at[0], final.at[0], final_send.at[0], final_recv.at[0], at(zx, yy, core, xx * 4 + zy))
    partner = jnp.where(zy != yy, jnp.where(yy < zy, core, 1 - core), 1 - core)
    to_turned = remote(sent.at[1], final.at[1], final_send.at[1], final_recv.at[1], at(xx, zy, partner, zx * 4 + yy))

    @pl.when(same_x)
    def _():
        final[0] = value

    @pl.when(jnp.logical_not(same_x))
    def _():
        sent[0] = value
        to_direct.start()

    turned[...] = flip_rows(value)
    flipped = jnp.concatenate(
        [
            jnp.concatenate([turned[pl.ds(16 * i + s, 4, stride=4), :] for i in range(6)], axis=1)
            for s in range(4)
        ],
        axis=0,
    )

    @pl.when(keep & jnp.logical_not(home))
    def _():
        final[1] = flipped

    @pl.when(jnp.logical_not(keep))
    def _():
        sent[1] = flipped
        to_turned.start()

    @pl.when(home)
    def _():
        for i, send in ((0, right), (1, left)):
            remote(part.at[16], extra_in.at[i], extra_send.at[0], extra_recv.at[i], at(xx, yy, core, send)).wait_recv()
        final[1] = scaled(part[16] + extra_in[0] + extra_in[1])

    @pl.when(jnp.logical_not(same_x))
    def _():
        to_direct.wait_recv()

    @pl.when(jnp.logical_not(keep))
    def _():
        to_turned.wait_recv()

    first = jnp.where(
        zy != yy,
        jnp.where(yy < zy, core, 1 - core),
        jnp.where(zx <= xx, core, 1 - core),
    )
    one, two = final[0], final[1]
    low = jnp.where(first == 0, one, two)
    high = jnp.where(first == 0, two, one)
    for a in range(4):
        out[a] = jnp.concatenate([low[4 * a : 4 * a + 4, :WINDOW], high[4 * a : 4 * a + 4, :WINDOW]], axis=0)

    @pl.when(jnp.logical_not(same_x))
    def _():
        to_direct.wait_send()

    @pl.when(jnp.logical_not(keep))
    def _():
        to_turned.wait_send()

    for copy in gathers:
        copy.wait_send()
    for i in range(8):
        remote(part.at[i], from_left.at[i], right_send.at[i], right_recv.at[i], at(xx, yy, core, right)).wait_send()
    for i in range(7):
        remote(part.at[i], from_right.at[i], left_send.at[i], left_recv.at[i], at(xx, yy, core, left)).wait_send()

    @pl.when(jnp.logical_not(home))
    def _():
        remote(part.at[16], extra_in.at[0], extra_send.at[0], extra_recv.at[0], at(xx, yy, core, right)).wait_send()


def body(x_tables, table, spectra, tilt_ranges):
    anywhere = pl.BlockSpec(memory_space=pl.ANY)
    f32, bf16 = jnp.float32, jnp.bfloat16
    dma = pltpu.SemaphoreType.DMA
    return pl.pallas_call(
        fused_kernel,
        out_shape=jax.ShapeDtypeStruct((4, 8, WINDOW), f32),
        in_specs=[anywhere] * 4,
        out_specs=pl.BlockSpec(memory_space=pltpu.VMEM),
        scratch_shapes=[
            pltpu.VMEM((4, 2, HALF, 256), bf16),
            pltpu.SMEM((4, 2), jnp.int32),
            pltpu.VMEM((LAGS, 8, 128), f32),
            pltpu.VMEM((2, 224, 256), bf16),
            pltpu.VMEM((128, 256), f32),
            pltpu.VMEM((HALF, 16, 128), f32),
            pltpu.VMEM((TILES, 16, 128), bf16),
            pltpu.VMEM((4, TILES, 16, 128), bf16),
            pltpu.VMEM((8, TILES, 16, 128), bf16),
            pltpu.VMEM((2, HALF, 288, 256), bf16),
            pltpu.VMEM((HALF, LAGS, 8, 128), f32),
            pltpu.VMEM((LAGS, LAGS, 8, 128), f32),
            pltpu.VMEM((88 * 8, 128), f32),
            pltpu.VMEM((17, 16, PADDED), f32),
            pltpu.VMEM((8, 16, PADDED), f32),
            pltpu.VMEM((7, 16, PADDED), f32),
            pltpu.VMEM((2, 16, PADDED), f32),
            pltpu.VMEM((2, 16, PADDED), f32),
            pltpu.VMEM((2, 16, PADDED), f32),
            pltpu.VMEM((96, 128), f32),
            dma((4,)),
            dma((4,)),
            dma((4,)),
            dma((4,)),
            dma((5,)),
            dma((8,)),
            dma((8,)),
            dma((7,)),
            dma((7,)),
            dma((1,)),
            dma((2,)),
            dma((2,)),
            dma((2,)),
        ],
        compiler_params=pltpu.CompilerParams(
            vmem_limit_bytes=60 * 1024 * 1024, collective_id=0, has_side_effects=True
        ),
    )(spectra, tilt_ranges, table, x_tables)


def solution(mesh):
    cols = mesh.shape["col"]
    inner = functools.partial(body, jnp.asarray(x_table(cols)), jnp.asarray(y_table()))
    return jax.shard_map(
        inner,
        mesh=mesh,
        in_specs=(P("row", None, None, "col"), P("row", None)),
        out_specs=P("row", "col", None),
        check_vma=False,
    )
```

```python
import functools
import math

import jax
import jax.numpy as jnp
import ml_dtypes
import numpy as np
from jax import lax
from jax.experimental import pallas as pl
from jax.experimental.pallas import tpu as pltpu
from jax.sharding import PartitionSpec as P

EDGE = 64
HALF = 33
REACH = 4
LAGS = 9
WINDOW = 729
PADDED = 768
TILES = HALF + 2
PIECE = 40
ROWS = 24
NT = (((1,), (1,)), ((), ()))


def split_np(x):
    high = x.astype(ml_dtypes.bfloat16)
    low = (x - high.astype(np.float64)).astype(ml_dtypes.bfloat16)
    return high, low


def y_table():
    freq = np.arange(EDGE)
    out = np.zeros((LAGS, 8, 128), np.float32)
    for i in range(LAGS):
        if i <= REACH:
            t = np.cos(2 * np.pi * freq * i / EDGE)
        else:
            t = np.sin(2 * np.pi * freq * (i - REACH) / EDGE)
        out[i, :, :EDGE] = t
        out[i, :4, EDGE:] = t
        out[i, 4:, EDGE:] = -t
    return out


def x_table(cols):
    out = np.zeros((cols, LAGS, ROWS, 2, 8, 4, 4), np.float64)
    for col in range(cols):
        for k in range(4):
            for lx in range(-REACH, REACH + 1):
                angle = 2 * np.pi * ((col * 4 + k) * lx % EDGE) / EDGE
                for r in range(ROWS // 4):
                    for s in range(4):
                        out[col, lx + REACH, r * 4 + s, 0, r, k, s] = math.cos(angle)
                        out[col, lx + REACH, r * 4 + s, 1, r, k, s] = -math.sin(angle)
    out = out.reshape(cols, LAGS * ROWS, 256)
    out = np.pad(out, ((0, 0), (0, 224 - LAGS * ROWS), (0, 0)))
    return np.stack(split_np(out), 1)


def z_coefs():
    weight = [1.0 if k in (0, 32) else 2.0 for k in range(HALF)]
    cos = [[weight[k] * math.cos(2 * math.pi * k * l / EDGE) for k in range(HALF)] for l in range(REACH + 1)]
    sin = [[weight[k] * math.sin(2 * math.pi * k * l / EDGE) for k in range(HALF)] for l in range(REACH + 1)]
    return cos, sin


def signed(freq_x):
    return jnp.where(freq_x < EDGE // 2, freq_x, freq_x - EDGE)


def observed(freq_z, freq_x, up, down):
    q = signed(freq_x)
    return 16 * freq_z <= jnp.where(q > 0, up, down) * jnp.abs(q)


def prepare(col, spectra, tilts, message, power, pieces):
    lanes = lax.broadcasted_iota(jnp.int32, (HALF, 256), 1)
    freq_z = lax.broadcasted_iota(jnp.int32, (HALF, 256), 0)
    freq_x = col * 4 + lanes // EDGE
    weight = jnp.where((freq_z == 0) | (freq_z == EDGE // 2), 1.0, 2.0).astype(jnp.float32)
    power[...] = jnp.zeros_like(power)
    row = lax.broadcasted_iota(jnp.int32, (16, 256), 0)
    lane = lax.broadcasted_iota(jnp.int32, (16, 256), 1)
    total = jnp.zeros((16, 128), jnp.float32)
    for s in range(4):
        mask = observed(freq_z, freq_x, tilts[0, s], tilts[1, s])
        real = jnp.where(mask, spectra[s, 0].astype(jnp.float32), 0.0)
        imag = jnp.where(mask, spectra[s, 1].astype(jnp.float32), 0.0)
        square = (real * real + imag * imag) * weight
        for p in range(3):
            power[PIECE * p : PIECE * p + HALF, :] = square
        chosen = jnp.where((row // 4 == lane // EDGE) & (row % 4 == s), 1.0, 0.0)
        total = total + lax.dot_general(
            chosen, power[...], NT, precision=lax.Precision.HIGHEST, preferred_element_type=jnp.float32
        )
        for k in range(4):
            part = slice(k * EDGE, (k + 1) * EDGE)
            pieces[:, k * 4 + s, :] = jnp.concatenate([real[:, part], imag[:, part]], axis=1)
    message[:HALF] = pieces[...].astype(jnp.bfloat16)
    lane = lax.broadcasted_iota(jnp.int32, (16, 128), 1)
    row = lax.broadcasted_iota(jnp.int32, (16, 128), 0)
    high = total.astype(jnp.bfloat16).astype(jnp.float32)
    rest = total - high
    mid = rest.astype(jnp.bfloat16).astype(jnp.float32)
    low = rest - mid
    third = lane // PIECE
    message[HALF] = jnp.where(third == 0, high, jnp.where(third == 1, mid, low)).astype(jnp.bfloat16)
    s = row % 4
    up, down = (
        jnp.where(s == 0, tilts[i, 0], jnp.where(s == 1, tilts[i, 1], jnp.where(s == 2, tilts[i, 2], tilts[i, 3])))
        for i in range(2)
    )
    at = lane - third * PIECE
    mask = observed(at, col * 4 + row // 4, up, down) & (at < HALF) & (third < 3)
    message[HALF + 1] = jnp.where(mask, 1.0, 0.0).astype(jnp.bfloat16)


def modulate(block, table, mod):
    def one(z, carry):
        base = block[z].astype(jnp.float32)
        turned = pltpu.roll(base, EDGE, 1)
        values = []
        for k in range(0, 4, 2):
            a, b = base[4 * k : 4 * k + 8], turned[4 * k : 4 * k + 8]
            for both in (
                jnp.where(first, a, pltpu.roll(b, 4, 0)),
                jnp.where(first, pltpu.roll(a, 4, 0), b),
            ):
                values += [both * table[i] for i in range(LAGS)]
        value = jnp.concatenate(values, axis=0)
        high = value.astype(jnp.bfloat16)
        mod[z, :, :128] = high
        mod[z, :, 128:] = (value - high.astype(jnp.float32)).astype(jnp.bfloat16)
        return carry

    first = lax.broadcasted_iota(jnp.int32, (8, 128), 0) < 4

    lax.fori_loop(0, HALF, one, 0, unroll=11)


def window_tile(own, mod, blocks, depth, quads, middle):
    lane_k = (lax.broadcasted_iota(jnp.int32, (8, 128), 1) // 4) % 4

    def diagonal(values):
        lane = jnp.concatenate([lane_k] * (values[0].shape[0] // 8), axis=0) if values[0].shape[0] > 8 else lane_k
        out = values[3]
        for k in (2, 1, 0):
            out = jnp.where(lane == k, values[k], out)
        return out

    def one(z, carry):
        tile = blocks(z)
        product = lax.dot_general(
            mod[z], jnp.concatenate([tile, tile], axis=1), NT, preferred_element_type=jnp.float32
        )
        depth[z] = diagonal([product[72 * k : 72 * k + 72] for k in range(4)]).reshape(LAGS, 8, 128)
        return carry

    lax.fori_loop(0, HALF, one, 0, unroll=11)

    middle()
    energies = []
    for own_tile, other in ((HALF, HALF + 1), (HALF + 1, HALF)):
        product = lax.dot_general(own[own_tile], blocks(other), NT, preferred_element_type=jnp.float32)
        picked = jnp.zeros((4, 128), jnp.float32)
        for k in range(4):
            picked = jnp.where(lane_k[:4] == k, product[4 * k : 4 * k + 4], picked)
        energies.append(jnp.concatenate([picked, jnp.zeros((4, 128), jnp.float32)], axis=0))

    cos, sin = z_coefs()

    def along_z(i, carry):
        value = [depth[z, i] for z in range(HALF)]
        even = [value[z] + value[32 - z] for z in range(16)] + [value[16]]
        odd = [value[z] - value[32 - z] for z in range(16)] + [value[16]]
        for lag in range(REACH + 1):
            source = even if lag % 2 == 0 else odd
            total = None
            for z in range(17):
                c = cos[lag][z]
                if z == 16 and lag % 2 == 1 or abs(c) < 1e-12:
                    continue
                term = source[z] * c
                total = term if total is None else total + term
            quads[lag, i] = total
        for lag in range(1, REACH + 1):
            source = odd if lag % 2 == 0 else even
            total = None
            for z in range(17):
                c = sin[lag][z]
                if z == 16 and lag % 2 == 0 or abs(c) < 1e-12:
                    continue
                term = source[z] * c
                total = term if total is None else total + term
            quads[REACH + lag, i] = total
        return carry

    lax.fori_loop(0, LAGS, along_z, 0)

    half = lax.broadcasted_iota(jnp.int32, (8, 128), 0) < 4

    def times_i(x):
        y = pltpu.roll(x, 4, 0)
        return jnp.where(half, -y, y)

    q = {}
    for ly in range(REACH + 1):
        for lz in range(REACH + 1):
            cc = quads[lz, ly]
            if ly == 0 and lz == 0:
                q[0, 0] = cc
            elif ly == 0:
                g = times_i(quads[REACH + lz, 0])
                q[0, lz], q[0, -lz] = cc + g, cc - g
            elif lz == 0:
                g = times_i(quads[0, REACH + ly])
                q[ly, 0], q[-ly, 0] = cc + g, cc - g
            else:
                ss = quads[REACH + lz, REACH + ly]
                sc = quads[lz, REACH + ly]
                cs = quads[REACH + lz, ly]
                p, m = cc - ss, cc + ss
                g, h = times_i(sc + cs), times_i(sc - cs)
                q[ly, lz], q[-ly, -lz] = p + g, p - g
                q[ly, -lz], q[-ly, lz] = m + h, m - h
    order = [q[ly, lz] for ly in range(-REACH, REACH + 1) for lz in range(-REACH, REACH + 1)] + energies
    order = order + [jnp.zeros((8, 128), jnp.float32)] * 5
    return order


def window_out(order_ref, xt, s):
    real = order_ref[pl.ds(s, 88, stride=8), :]
    imag = order_ref[pl.ds(4 + s, 88, stride=8), :]
    value = jnp.concatenate([real, imag], axis=1)
    high = value.astype(jnp.bfloat16)
    low = (value - high.astype(jnp.float32)).astype(jnp.bfloat16)
    x_high, x_low = xt[0], xt[1]
    dot = functools.partial(lax.dot_general, dimension_numbers=NT, preferred_element_type=jnp.float32)
    out = dot(x_high, high) + (dot(x_low, high) + dot(x_high, low))
    pieces = [out[ROWS * i : ROWS * i + ROWS, :81] for i in range(LAGS)]
    energy = out[ROWS * REACH : ROWS * REACH + ROWS, 81:83]
    fill = jnp.zeros((ROWS, PADDED - WINDOW - 2), jnp.float32)
    return jnp.concatenate(pieces + [energy, fill], axis=1)


def write_part(x, xx, yy, order, xt, part):
    first = lax.broadcasted_iota(jnp.int32, (8, PADDED), 0) < 4
    for pair in range(2):
        a, b = window_out(order, xt, 2 * pair), window_out(order, xt, 2 * pair + 1)
        blocks = []
        for i in range(0, ROWS, 8):
            upper, lower = a[i : i + 8], b[i : i + 8]
            blocks.append(jnp.where(first, upper, pltpu.roll(lower, 4, 0)))
            blocks.append(jnp.where(first, pltpu.roll(upper, 4, 0), lower))
        for y in range(4):
            swap = (yy == y) & (x < xx)
            part[x * 4 + y, 8 * pair : 8 * pair + 8, :] = jnp.where(swap, blocks[4], blocks[y])

        @pl.when(x == xx)
        def _():
            part[16, 8 * pair : 8 * pair + 8, :] = blocks[4]


def flip_rows(rows):
    moved = pltpu.roll(rows, PADDED - WINDOW, 1)
    stacked = jnp.concatenate([moved[:, 128 * (5 - i) : 128 * (6 - i)] for i in range(6)], axis=0)
    row = lax.broadcasted_iota(jnp.int32, (128, 128), 0)
    lane = lax.broadcasted_iota(jnp.int32, (128, 128), 1)
    swap = jnp.where(row + lane == 127, 1.0, 0.0).astype(jnp.bfloat16)
    out = None
    for _ in range(3):
        high = stacked.astype(jnp.bfloat16)
        stacked = stacked - high.astype(jnp.float32)
        part = jnp.dot(high, swap, preferred_element_type=jnp.float32)
        out = part if out is None else out + part
    return out


def fused_kernel(
    spectra_any, tilts_any, table_any, tables_any, out,
    spectra, tilts, table, xt, power, pieces, own, mods, lanes, mod, depth, quads, order,
    part, merge, chain, extra_merge, extra_chain, sent, final, turned,
    local_sem, x_send, x_recv, y_send, y_recv, merge_send, merge_recv, chain_send, chain_recv,
    extra_send, extra_merge_recv, extra_chain_recv, final_send, final_recv,
):
    row = lax.axis_index("row")
    z = lax.axis_index("col")
    xx, yy, core = row // 8, (row // 2) % 4, row % 2
    zx, zy = z // 4, z % 4
    chip = xx * 4 + yy

    def at(x, y, c, depth_z):
        return {"row": (x * 4 + y) * 2 + c, "col": depth_z}

    def along(offset):
        return at(xx, yy, core, lax.rem(z + offset, 16))

    locals_ = [
        pltpu.make_async_copy(spectra_any, spectra, local_sem.at[0]),
        pltpu.make_async_copy(tilts_any, tilts, local_sem.at[1]),
        pltpu.make_async_copy(table_any, table, local_sem.at[2]),
        pltpu.make_async_copy(tables_any.at[z], xt, local_sem.at[3]),
    ]
    for copy in locals_:
        copy.start()

    barrier = pltpu.get_barrier_semaphore()

    def greet(target):
        pl.semaphore_signal(barrier, inc=1, device_id=target, device_id_type=pl.DeviceIdType.MESH)

    for i in range(1, 4):
        greet(at(lax.rem(xx + i, 4), yy, core, z))
        greet(at(xx, lax.rem(yy + i, 4), 0, z))
        greet(at(xx, lax.rem(yy + i, 4), 1, z))
    greet(at(xx, yy, 1 - core, z))
    for offset in (1, 15, 2, 14):
        greet(along(offset))

    @pl.when(zx != xx)
    def _():
        greet(at(zx, yy, core, xx * 4 + zy))

    @pl.when(zy != yy)
    def _():
        greet(at(xx, zy, 0, zx * 4 + yy))
        greet(at(xx, zy, 1, zx * 4 + yy))

    locals_[0].wait()
    locals_[1].wait()
    prepare(z, spectra, tilts, own, power, pieces)
    count = 14 + jnp.where(zx != xx, 1, 0) + jnp.where(zy != yy, 2, 0)
    pl.semaphore_wait(barrier, count)

    def remote(src, dst, send, recv, target):
        return pltpu.make_async_remote_copy(
            src_ref=src, dst_ref=dst, send_sem=send, recv_sem=recv,
            device_id=target, device_id_type=pl.DeviceIdType.MESH,
        )

    gathers = []
    for i in (2, 1, 3):
        y = lax.rem(yy + i, 4)
        there = jnp.where(y < yy, core, 1 - core)
        gathers.append(remote(own, lanes.at[yy], y_send.at[i], y_recv.at[yy], at(xx, y, there, z)))
    gathers.append(remote(own, lanes.at[4], y_send.at[0], y_recv.at[4], at(xx, yy, 1 - core, z)))
    for i in (1, 3, 2):
        x = lax.rem(xx + i, 4)
        gathers.append(remote(own, mods.at[xx], x_send.at[i], x_recv.at[xx], at(x, yy, core, z)))
    for copy in gathers:
        copy.start()

    lanes[yy] = own[...]
    mods[xx] = own[...]
    lanes[5:8] = jnp.zeros((3, TILES, 16, 128), jnp.bfloat16)
    locals_[2].wait()
    modulate(own, table, mod.at[0])
    locals_[3].wait()

    def wait_lane(slot):
        remote(own, lanes.at[slot], y_send.at[0], y_recv.at[slot], at(xx, yy, 1 - core, z)).wait_recv()

    for i in range(1, 4):
        wait_lane(lax.rem(yy + i, 4))
    wait_lane(4)

    near_hop, far_hop = (1, 15), (2, 14)

    def merging(side, i, chunk):
        return remote(
            part.at[chunk], merge.at[side, i], merge_send.at[side, i], merge_recv.at[side, i], along(near_hop[side])
        )

    def chaining(side, i, chunk):
        return remote(
            part.at[chunk], chain.at[side, i], chain_send.at[side, i], chain_recv.at[side, i], along(far_hop[side])
        )

    def extra_merging(side):
        return remote(
            part.at[16], extra_merge.at[side], extra_send.at[0], extra_merge_recv.at[side], along(near_hop[side])
        )

    def extra_chaining(side):
        return remote(
            part.at[16], extra_chain.at[side], extra_send.at[0], extra_chain_recv.at[side], along(far_hop[side])
        )

    def spread(x):
        for k in range(4):
            chunk = x * 4 + k
            ahead = lax.rem(chunk + 16 - z, 16)
            odd = lax.rem(ahead, 2) == 1
            for side, here, gap in ((0, odd & (ahead < 8), ahead), (1, odd & (ahead > 8), 16 - ahead)):
                @pl.when(here)
                def _():
                    merging(side, gap // 2, chunk).start()

                    @pl.when(chunk == chip)
                    def _():
                        extra_merging(side).start()

    def step(side, gap):
        longest = 8 - 2 * side
        chunk = lax.rem(z + (gap, 16 - gap)[side], 16)
        order_at = (longest - gap) // 2
        merged, chained = gap < 8, gap < longest
        if merged:
            merging(side, gap // 2, chunk).wait_recv()
            part[chunk] = part[chunk] + merge[side, gap // 2]
        if chained:
            chaining(side, order_at - 1, chunk).wait_recv()
            part[chunk] = part[chunk] + chain[side, order_at - 1]
        chaining(side, order_at, chunk).start()

        @pl.when(chunk == chip)
        def _():
            if merged:
                extra_merging(side).wait_recv()
                part[16] = part[16] + extra_merge[side]
            if chained:
                extra_chaining(side).wait_recv()
                part[16] = part[16] + extra_chain[side]
            extra_chaining(side).start()

    second = jnp.where(zy < 2, 1, 3)

    def task(q, carry):
        turn = jnp.where(q == 0, 2, jnp.where(q == 1, second, jnp.where(q == 2, 4 - second, 0)))
        x = lax.rem(zx + turn, 4)

        @pl.when(x != xx)
        def _():
            remote(own, mods.at[x], x_send.at[0], x_recv.at[x], at(xx, yy, 1 - core, z)).wait_recv()
            modulate(mods.at[x], table, mod.at[1])

        def middle():
            for at_q, gap in ((2, 6), (3, 4)):
                @pl.when(q == at_q)
                def _():
                    step(0, gap)
                    step(1, gap)

        def blocks(k):
            return lanes[:, k].reshape(128, 128)

        rows = window_tile(mods.at[x], mod.at[jnp.where(x == xx, 0, 1)], blocks, depth, quads, middle)
        order[...] = jnp.concatenate(rows, axis=0)
        write_part(x, xx, yy, order, xt, part)

        spread(x)

        @pl.when(q == 0)
        def _():
            step(0, 8)

        return carry

    lax.fori_loop(0, 4, task, 0)
    step(0, 2)
    step(1, 2)
    for side in range(2):
        merging(side, 0, z).wait_recv()
        chaining(side, 3 - side, z).wait_recv()

    def scaled(total):
        return total / jnp.sqrt(total[:, WINDOW : WINDOW + 1] * total[:, WINDOW + 1 : WINDOW + 2])

    value = scaled(part[z] + (merge[0, 0] + merge[1, 0]) + (chain[0, 3] + chain[1, 2]))
    same_x = zx == xx
    home = z == chip
    keep = (zy == yy) & (zx >= xx)
    to_direct = remote(sent.at[0], final.at[0], final_send.at[0], final_recv.at[0], at(zx, yy, core, xx * 4 + zy))
    partner = jnp.where(zy != yy, jnp.where(yy < zy, core, 1 - core), 1 - core)
    to_turned = remote(sent.at[1], final.at[1], final_send.at[1], final_recv.at[1], at(xx, zy, partner, zx * 4 + yy))

    @pl.when(same_x)
    def _():
        final[0] = value

    @pl.when(jnp.logical_not(same_x))
    def _():
        sent[0] = value
        to_direct.start()

    turned[...] = flip_rows(value)
    flipped = jnp.concatenate(
        [
            jnp.concatenate([turned[pl.ds(16 * i + s, 4, stride=4), :] for i in range(6)], axis=1)
            for s in range(4)
        ],
        axis=0,
    )

    @pl.when(keep & jnp.logical_not(home))
    def _():
        final[1] = flipped

    @pl.when(jnp.logical_not(keep))
    def _():
        sent[1] = flipped
        to_turned.start()

    @pl.when(home)
    def _():
        for side in range(2):
            extra_merging(side).wait_recv()
            extra_chaining(side).wait_recv()
        final[1] = scaled(part[16] + (extra_merge[0] + extra_merge[1]) + (extra_chain[0] + extra_chain[1]))

    @pl.when(jnp.logical_not(same_x))
    def _():
        to_direct.wait_recv()

    @pl.when(jnp.logical_not(keep))
    def _():
        to_turned.wait_recv()

    first = jnp.where(
        zy != yy,
        jnp.where(yy < zy, core, 1 - core),
        jnp.where(zx <= xx, core, 1 - core),
    )
    one, two = final[0], final[1]
    low = jnp.where(first == 0, one, two)
    high = jnp.where(first == 0, two, one)
    for a in range(4):
        out[a] = jnp.concatenate([low[4 * a : 4 * a + 4, :WINDOW], high[4 * a : 4 * a + 4, :WINDOW]], axis=0)

    @pl.when(jnp.logical_not(same_x))
    def _():
        to_direct.wait_send()

    @pl.when(jnp.logical_not(keep))
    def _():
        to_turned.wait_send()

    for copy in gathers:
        copy.wait_send()
    for side in range(2):
        for i in range(4):
            merging(side, i, z).wait_send()
        for i in range(4 - side):
            chaining(side, i, z).wait_send()

    @pl.when(jnp.logical_not(home))
    def _():
        extra_merging(0).wait_send()


def body(x_tables, table, spectra, tilt_ranges):
    anywhere = pl.BlockSpec(memory_space=pl.ANY)
    f32, bf16 = jnp.float32, jnp.bfloat16
    dma = pltpu.SemaphoreType.DMA
    return pl.pallas_call(
        fused_kernel,
        out_shape=jax.ShapeDtypeStruct((4, 8, WINDOW), f32),
        in_specs=[anywhere] * 4,
        out_specs=pl.BlockSpec(memory_space=pltpu.VMEM),
        scratch_shapes=[
            pltpu.VMEM((4, 2, HALF, 256), bf16),
            pltpu.SMEM((2, 4), jnp.int32),
            pltpu.VMEM((LAGS, 8, 128), f32),
            pltpu.VMEM((2, 224, 256), bf16),
            pltpu.VMEM((128, 256), f32),
            pltpu.VMEM((HALF, 16, 128), f32),
            pltpu.VMEM((TILES, 16, 128), bf16),
            pltpu.VMEM((4, TILES, 16, 128), bf16),
            pltpu.VMEM((8, TILES, 16, 128), bf16),
            pltpu.VMEM((2, HALF, 288, 256), bf16),
            pltpu.VMEM((HALF, LAGS, 8, 128), f32),
            pltpu.VMEM((LAGS, LAGS, 8, 128), f32),
            pltpu.VMEM((88 * 8, 128), f32),
            pltpu.VMEM((17, 16, PADDED), f32),
            pltpu.VMEM((2, 4, 16, PADDED), f32),
            pltpu.VMEM((2, 4, 16, PADDED), f32),
            pltpu.VMEM((2, 16, PADDED), f32),
            pltpu.VMEM((2, 16, PADDED), f32),
            pltpu.VMEM((2, 16, PADDED), f32),
            pltpu.VMEM((2, 16, PADDED), f32),
            pltpu.VMEM((96, 128), f32),
            dma((4,)),
            dma((4,)),
            dma((4,)),
            dma((4,)),
            dma((5,)),
            dma((2, 4)),
            dma((2, 4)),
            dma((2, 4)),
            dma((2, 4)),
            dma((1,)),
            dma((2,)),
            dma((2,)),
            dma((2,)),
            dma((2,)),
        ],
        compiler_params=pltpu.CompilerParams(
            vmem_limit_bytes=60 * 1024 * 1024, collective_id=0, has_side_effects=True
        ),
    )(spectra, tilt_ranges.T, table, x_tables)


def solution(mesh):
    cols = mesh.shape["col"]
    inner = functools.partial(body, jnp.asarray(x_table(cols)), jnp.asarray(y_table()))
    return jax.shard_map(
        inner,
        mesh=mesh,
        in_specs=(P("row", None, None, "col"), P("row", None)),
        out_specs=P("row", "col", None),
        check_vma=False,
    )
```

```python
import functools
import math

import jax
import jax.numpy as jnp
import ml_dtypes
import numpy as np
from jax import lax
from jax.experimental import pallas as pl
from jax.experimental.pallas import tpu as pltpu
from jax.sharding import PartitionSpec as P

EDGE = 64
HALF = 33
REACH = 4
LAGS = 9
WINDOW = 729
PADDED = 768
TILES = HALF + 2
PIECE = 40
PARTS = ((0, 22), (22, HALF))
SPANS = ((0, 22), (22, TILES))
ROWS = 24
NT = (((1,), (1,)), ((), ()))


def split_np(x):
    high = x.astype(ml_dtypes.bfloat16)
    low = (x - high.astype(np.float64)).astype(ml_dtypes.bfloat16)
    return high, low


def y_table():
    freq = np.arange(EDGE)
    out = np.zeros((LAGS, 8, 128), np.float32)
    for i in range(LAGS):
        if i <= REACH:
            t = np.cos(2 * np.pi * freq * i / EDGE)
        else:
            t = np.sin(2 * np.pi * freq * (i - REACH) / EDGE)
        out[i, :, :EDGE] = t
        out[i, :4, EDGE:] = t
        out[i, 4:, EDGE:] = -t
    return out


def x_table(cols):
    out = np.zeros((cols, LAGS, ROWS, 2, 8, 4, 4), np.float64)
    for col in range(cols):
        for k in range(4):
            for lx in range(-REACH, REACH + 1):
                angle = 2 * np.pi * ((col * 4 + k) * lx % EDGE) / EDGE
                for r in range(ROWS // 4):
                    for s in range(4):
                        out[col, lx + REACH, r * 4 + s, 0, r, k, s] = math.cos(angle)
                        out[col, lx + REACH, r * 4 + s, 1, r, k, s] = -math.sin(angle)
    out = out.reshape(cols, LAGS * ROWS, 256)
    out = np.pad(out, ((0, 0), (0, 224 - LAGS * ROWS), (0, 0)))
    return np.stack(split_np(out), 1)


def z_coefs():
    weight = [1.0 if k in (0, 32) else 2.0 for k in range(HALF)]
    cos = [[weight[k] * math.cos(2 * math.pi * k * l / EDGE) for k in range(HALF)] for l in range(REACH + 1)]
    sin = [[weight[k] * math.sin(2 * math.pi * k * l / EDGE) for k in range(HALF)] for l in range(REACH + 1)]
    return cos, sin


def signed(freq_x):
    return jnp.where(freq_x < EDGE // 2, freq_x, freq_x - EDGE)


def observed(freq_z, freq_x, up, down):
    q = signed(freq_x)
    return 16 * freq_z <= jnp.where(q > 0, up, down) * jnp.abs(q)


def prepare_first(col, spectra, tilts, message, squares, pieces):
    lanes = lax.broadcasted_iota(jnp.int32, (HALF, 256), 1)
    freq_z = lax.broadcasted_iota(jnp.int32, (HALF, 256), 0)
    freq_x = col * 4 + lanes // EDGE
    weight = jnp.where((freq_z == 0) | (freq_z == EDGE // 2), 1.0, 2.0).astype(jnp.float32)
    for s in range(4):
        mask = observed(freq_z, freq_x, tilts[0, s], tilts[1, s])
        real = jnp.where(mask, spectra[s, 0].astype(jnp.float32), 0.0)
        imag = jnp.where(mask, spectra[s, 1].astype(jnp.float32), 0.0)
        squares[s] = (real * real + imag * imag) * weight
        for k in range(4):
            part = slice(k * EDGE, (k + 1) * EDGE)
            pieces[:, k * 4 + s, :] = jnp.concatenate([real[:, part], imag[:, part]], axis=1)
    first, last = PARTS[0]
    message[first:last] = pieces[first:last].astype(jnp.bfloat16)


def prepare_second(col, tilts, message, squares, power, pieces):
    first, last = PARTS[1]
    message[first:last] = pieces[first:last].astype(jnp.bfloat16)
    power[...] = jnp.zeros_like(power)
    row = lax.broadcasted_iota(jnp.int32, (16, 256), 0)
    lane = lax.broadcasted_iota(jnp.int32, (16, 256), 1)
    total = jnp.zeros((16, 128), jnp.float32)
    for s in range(4):
        for p in range(3):
            power[PIECE * p : PIECE * p + HALF, :] = squares[s]
        chosen = jnp.where((row // 4 == lane // EDGE) & (row % 4 == s), 1.0, 0.0)
        total = total + lax.dot_general(
            chosen, power[...], NT, precision=lax.Precision.HIGHEST, preferred_element_type=jnp.float32
        )
    lane = lax.broadcasted_iota(jnp.int32, (16, 128), 1)
    row = lax.broadcasted_iota(jnp.int32, (16, 128), 0)
    high = total.astype(jnp.bfloat16).astype(jnp.float32)
    rest = total - high
    mid = rest.astype(jnp.bfloat16).astype(jnp.float32)
    low = rest - mid
    third = lane // PIECE
    message[HALF] = jnp.where(third == 0, high, jnp.where(third == 1, mid, low)).astype(jnp.bfloat16)
    s = row % 4
    up, down = (
        jnp.where(s == 0, tilts[i, 0], jnp.where(s == 1, tilts[i, 1], jnp.where(s == 2, tilts[i, 2], tilts[i, 3])))
        for i in range(2)
    )
    at = lane - third * PIECE
    mask = observed(at, col * 4 + row // 4, up, down) & (at < HALF) & (third < 3)
    message[HALF + 1] = jnp.where(mask, 1.0, 0.0).astype(jnp.bfloat16)


def modulate(block, table, mod, part):
    def one(z, carry):
        base = block[z].astype(jnp.float32)
        turned = pltpu.roll(base, EDGE, 1)
        values = []
        for k in range(0, 4, 2):
            a, b = base[4 * k : 4 * k + 8], turned[4 * k : 4 * k + 8]
            for both in (
                jnp.where(first, a, pltpu.roll(b, 4, 0)),
                jnp.where(first, pltpu.roll(a, 4, 0), b),
            ):
                values += [both * table[i] for i in range(LAGS)]
        value = jnp.concatenate(values, axis=0)
        high = value.astype(jnp.bfloat16)
        mod[z, :, :128] = high
        mod[z, :, 128:] = (value - high.astype(jnp.float32)).astype(jnp.bfloat16)
        return carry

    first = lax.broadcasted_iota(jnp.int32, (8, 128), 0) < 4

    lax.fori_loop(*part, one, 0, unroll=11)


def window_tile(own, mod, blocks, depth, quads, middle, ready):
    lane_k = (lax.broadcasted_iota(jnp.int32, (8, 128), 1) // 4) % 4

    def diagonal(values):
        lane = jnp.concatenate([lane_k] * (values[0].shape[0] // 8), axis=0) if values[0].shape[0] > 8 else lane_k
        out = values[3]
        for k in (2, 1, 0):
            out = jnp.where(lane == k, values[k], out)
        return out

    def one(z, carry):
        tile = blocks(z)
        product = lax.dot_general(
            mod[z], jnp.concatenate([tile, tile], axis=1), NT, preferred_element_type=jnp.float32
        )
        depth[z] = diagonal([product[72 * k : 72 * k + 72] for k in range(4)]).reshape(LAGS, 8, 128)
        return carry

    for i, part in enumerate(PARTS):
        ready(i)
        lax.fori_loop(*part, one, 0, unroll=11)

    middle()
    energies = []
    for own_tile, other in ((HALF, HALF + 1), (HALF + 1, HALF)):
        product = lax.dot_general(own[own_tile], blocks(other), NT, preferred_element_type=jnp.float32)
        picked = jnp.zeros((4, 128), jnp.float32)
        for k in range(4):
            picked = jnp.where(lane_k[:4] == k, product[4 * k : 4 * k + 4], picked)
        energies.append(jnp.concatenate([picked, jnp.zeros((4, 128), jnp.float32)], axis=0))

    cos, sin = z_coefs()

    def along_z(i, carry):
        value = [depth[z, i] for z in range(HALF)]
        even = [value[z] + value[32 - z] for z in range(16)] + [value[16]]
        odd = [value[z] - value[32 - z] for z in range(16)] + [value[16]]
        for lag in range(REACH + 1):
            source = even if lag % 2 == 0 else odd
            total = None
            for z in range(17):
                c = cos[lag][z]
                if z == 16 and lag % 2 == 1 or abs(c) < 1e-12:
                    continue
                term = source[z] * c
                total = term if total is None else total + term
            quads[lag, i] = total
        for lag in range(1, REACH + 1):
            source = odd if lag % 2 == 0 else even
            total = None
            for z in range(17):
                c = sin[lag][z]
                if z == 16 and lag % 2 == 0 or abs(c) < 1e-12:
                    continue
                term = source[z] * c
                total = term if total is None else total + term
            quads[REACH + lag, i] = total
        return carry

    lax.fori_loop(0, LAGS, along_z, 0)

    half = lax.broadcasted_iota(jnp.int32, (8, 128), 0) < 4

    def times_i(x):
        y = pltpu.roll(x, 4, 0)
        return jnp.where(half, -y, y)

    q = {}
    for ly in range(REACH + 1):
        for lz in range(REACH + 1):
            cc = quads[lz, ly]
            if ly == 0 and lz == 0:
                q[0, 0] = cc
            elif ly == 0:
                g = times_i(quads[REACH + lz, 0])
                q[0, lz], q[0, -lz] = cc + g, cc - g
            elif lz == 0:
                g = times_i(quads[0, REACH + ly])
                q[ly, 0], q[-ly, 0] = cc + g, cc - g
            else:
                ss = quads[REACH + lz, REACH + ly]
                sc = quads[lz, REACH + ly]
                cs = quads[REACH + lz, ly]
                p, m = cc - ss, cc + ss
                g, h = times_i(sc + cs), times_i(sc - cs)
                q[ly, lz], q[-ly, -lz] = p + g, p - g
                q[ly, -lz], q[-ly, lz] = m + h, m - h
    order = [q[ly, lz] for ly in range(-REACH, REACH + 1) for lz in range(-REACH, REACH + 1)] + energies
    order = order + [jnp.zeros((8, 128), jnp.float32)] * 5
    return order


def window_out(order_ref, xt, s):
    real = order_ref[pl.ds(s, 88, stride=8), :]
    imag = order_ref[pl.ds(4 + s, 88, stride=8), :]
    value = jnp.concatenate([real, imag], axis=1)
    high = value.astype(jnp.bfloat16)
    low = (value - high.astype(jnp.float32)).astype(jnp.bfloat16)
    x_high, x_low = xt[0], xt[1]
    dot = functools.partial(lax.dot_general, dimension_numbers=NT, preferred_element_type=jnp.float32)
    out = dot(x_high, high) + (dot(x_low, high) + dot(x_high, low))
    pieces = [out[ROWS * i : ROWS * i + ROWS, :81] for i in range(LAGS)]
    energy = out[ROWS * REACH : ROWS * REACH + ROWS, 81:83]
    fill = jnp.zeros((ROWS, PADDED - WINDOW - 2), jnp.float32)
    return jnp.concatenate(pieces + [energy, fill], axis=1)


def write_part(x, xx, yy, order, xt, part):
    first = lax.broadcasted_iota(jnp.int32, (8, PADDED), 0) < 4
    for pair in range(2):
        a, b = window_out(order, xt, 2 * pair), window_out(order, xt, 2 * pair + 1)
        blocks = []
        for i in range(0, ROWS, 8):
            upper, lower = a[i : i + 8], b[i : i + 8]
            blocks.append(jnp.where(first, upper, pltpu.roll(lower, 4, 0)))
            blocks.append(jnp.where(first, pltpu.roll(upper, 4, 0), lower))
        for y in range(4):
            swap = (yy == y) & (x < xx)
            part[x * 4 + y, 8 * pair : 8 * pair + 8, :] = jnp.where(swap, blocks[4], blocks[y])

        @pl.when(x == xx)
        def _():
            part[16, 8 * pair : 8 * pair + 8, :] = blocks[4]


def flip_rows(rows):
    moved = pltpu.roll(rows, PADDED - WINDOW, 1)
    stacked = jnp.concatenate([moved[:, 128 * (5 - i) : 128 * (6 - i)] for i in range(6)], axis=0)
    row = lax.broadcasted_iota(jnp.int32, (128, 128), 0)
    lane = lax.broadcasted_iota(jnp.int32, (128, 128), 1)
    swap = jnp.where(row + lane == 127, 1.0, 0.0).astype(jnp.bfloat16)
    out = None
    for _ in range(3):
        high = stacked.astype(jnp.bfloat16)
        stacked = stacked - high.astype(jnp.float32)
        part = jnp.dot(high, swap, preferred_element_type=jnp.float32)
        out = part if out is None else out + part
    return out


def fused_kernel(
    spectra_any, tilts_any, table_any, tables_any, out,
    spectra, tilts, table, xt, squares, power, pieces, own, mods, lanes, mod, depth, quads, order,
    part, merge, chain, extra_merge, extra_chain, sent, final, turned,
    local_sem, x_send, x_recv, y_send, y_recv, merge_send, merge_recv, chain_send, chain_recv,
    extra_send, extra_merge_recv, extra_chain_recv, final_send, final_recv,
):
    row = lax.axis_index("row")
    z = lax.axis_index("col")
    xx, yy, core = row // 8, (row // 2) % 4, row % 2
    zx, zy = z // 4, z % 4
    chip = xx * 4 + yy

    def at(x, y, c, depth_z):
        return {"row": (x * 4 + y) * 2 + c, "col": depth_z}

    def along(offset):
        return at(xx, yy, core, lax.rem(z + offset, 16))

    locals_ = [
        pltpu.make_async_copy(spectra_any, spectra, local_sem.at[0]),
        pltpu.make_async_copy(tilts_any, tilts, local_sem.at[1]),
        pltpu.make_async_copy(table_any, table, local_sem.at[2]),
        pltpu.make_async_copy(tables_any.at[z], xt, local_sem.at[3]),
    ]
    for copy in locals_:
        copy.start()

    barrier = pltpu.get_barrier_semaphore()

    def greet(target):
        pl.semaphore_signal(barrier, inc=1, device_id=target, device_id_type=pl.DeviceIdType.MESH)

    for i in range(1, 4):
        greet(at(lax.rem(xx + i, 4), yy, core, z))
        greet(at(xx, lax.rem(yy + i, 4), 0, z))
        greet(at(xx, lax.rem(yy + i, 4), 1, z))
    greet(at(xx, yy, 1 - core, z))
    for offset in (1, 15, 2, 14):
        greet(along(offset))

    @pl.when(zx != xx)
    def _():
        greet(at(zx, yy, core, xx * 4 + zy))

    @pl.when(zy != yy)
    def _():
        greet(at(xx, zy, 0, zx * 4 + yy))
        greet(at(xx, zy, 1, zx * 4 + yy))

    locals_[0].wait()
    locals_[1].wait()
    prepare_first(z, spectra, tilts, own, squares, pieces)
    count = 14 + jnp.where(zx != xx, 1, 0) + jnp.where(zy != yy, 2, 0)
    pl.semaphore_wait(barrier, count)

    def remote(src, dst, send, recv, target):
        return pltpu.make_async_remote_copy(
            src_ref=src, dst_ref=dst, send_sem=send, recv_sem=recv,
            device_id=target, device_id_type=pl.DeviceIdType.MESH,
        )

    gathers = []
    for i, span in enumerate(SPANS):
        if i == 1:
            prepare_second(z, tilts, own, squares, power, pieces)
        span = slice(*span)
        ready_now = []
        for n in (2, 1, 3):
            y = lax.rem(yy + n, 4)
            there = jnp.where(y < yy, core, 1 - core)
            ready_now.append(
                remote(own.at[span], lanes.at[yy, span], y_send.at[i, n], y_recv.at[i, yy], at(xx, y, there, z))
            )
        ready_now.append(
            remote(own.at[span], lanes.at[4, span], y_send.at[i, 0], y_recv.at[i, 4], at(xx, yy, 1 - core, z))
        )
        for n in (1, 3, 2):
            x = lax.rem(xx + n, 4)
            ready_now.append(
                remote(own.at[span], mods.at[xx, span], x_send.at[i, n], x_recv.at[i, xx], at(x, yy, core, z))
            )
        for copy in ready_now:
            copy.start()
        gathers += ready_now

    lanes[yy] = own[...]
    mods[xx] = own[...]
    lanes[5:8] = jnp.zeros((3, TILES, 16, 128), jnp.bfloat16)
    locals_[2].wait()
    modulate(own, table, mod.at[0], (0, HALF))
    locals_[3].wait()

    def wait_lane(i, slot):
        span = slice(*SPANS[i])
        remote(
            own.at[span], lanes.at[slot, span], y_send.at[i, 0], y_recv.at[i, slot], at(xx, yy, 1 - core, z)
        ).wait_recv()

    near_hop, far_hop = (1, 15), (2, 14)

    def merging(side, i, chunk):
        return remote(
            part.at[chunk], merge.at[side, i], merge_send.at[side, i], merge_recv.at[side, i], along(near_hop[side])
        )

    def chaining(side, i, chunk):
        return remote(
            part.at[chunk], chain.at[side, i], chain_send.at[side, i], chain_recv.at[side, i], along(far_hop[side])
        )

    def extra_merging(side):
        return remote(
            part.at[16], extra_merge.at[side], extra_send.at[0], extra_merge_recv.at[side], along(near_hop[side])
        )

    def extra_chaining(side):
        return remote(
            part.at[16], extra_chain.at[side], extra_send.at[0], extra_chain_recv.at[side], along(far_hop[side])
        )

    def spread(x):
        for k in range(4):
            chunk = x * 4 + k
            ahead = lax.rem(chunk + 16 - z, 16)
            odd = lax.rem(ahead, 2) == 1
            for side, here, gap in ((0, odd & (ahead < 8), ahead), (1, odd & (ahead > 8), 16 - ahead)):
                @pl.when(here)
                def _():
                    merging(side, gap // 2, chunk).start()

                    @pl.when(chunk == chip)
                    def _():
                        extra_merging(side).start()

    def step(side, gap):
        longest = 8 - 2 * side
        chunk = lax.rem(z + (gap, 16 - gap)[side], 16)
        order_at = (longest - gap) // 2
        merged, chained = gap < 8, gap < longest
        if merged:
            merging(side, gap // 2, chunk).wait_recv()
            part[chunk] = part[chunk] + merge[side, gap // 2]
        if chained:
            chaining(side, order_at - 1, chunk).wait_recv()
            part[chunk] = part[chunk] + chain[side, order_at - 1]
        chaining(side, order_at, chunk).start()

        @pl.when(chunk == chip)
        def _():
            if merged:
                extra_merging(side).wait_recv()
                part[16] = part[16] + extra_merge[side]
            if chained:
                extra_chaining(side).wait_recv()
                part[16] = part[16] + extra_chain[side]
            extra_chaining(side).start()

    second = jnp.where(zy < 2, 1, 3)

    def task(q, carry):
        turn = jnp.where(q == 0, 2, jnp.where(q == 1, second, jnp.where(q == 2, 4 - second, 0)))
        x = lax.rem(zx + turn, 4)

        def ready(i):
            @pl.when(x != xx)
            def _():
                span = slice(*SPANS[i])
                remote(
                    own.at[span], mods.at[x, span], x_send.at[i, 0], x_recv.at[i, x], at(xx, yy, 1 - core, z)
                ).wait_recv()
                modulate(mods.at[x], table, mod.at[1], PARTS[i])

            @pl.when(q == 0)
            def _():
                for n in range(1, 4):
                    wait_lane(i, lax.rem(yy + n, 4))
                wait_lane(i, 4)

        def middle():
            for at_q, gap in ((2, 6), (3, 4)):
                @pl.when(q == at_q)
                def _():
                    step(0, gap)
                    step(1, gap)

        def blocks(k):
            return lanes[:, k].reshape(128, 128)

        rows = window_tile(mods.at[x], mod.at[jnp.where(x == xx, 0, 1)], blocks, depth, quads, middle, ready)
        order[...] = jnp.concatenate(rows, axis=0)
        write_part(x, xx, yy, order, xt, part)

        spread(x)

        @pl.when(q == 0)
        def _():
            step(0, 8)

        return carry

    lax.fori_loop(0, 4, task, 0)
    step(0, 2)
    step(1, 2)
    for side in range(2):
        merging(side, 0, z).wait_recv()
        chaining(side, 3 - side, z).wait_recv()

    def scaled(total):
        return total / jnp.sqrt(total[:, WINDOW : WINDOW + 1] * total[:, WINDOW + 1 : WINDOW + 2])

    value = scaled(part[z] + (merge[0, 0] + merge[1, 0]) + (chain[0, 3] + chain[1, 2]))
    same_x = zx == xx
    home = z == chip
    keep = (zy == yy) & (zx >= xx)
    to_direct = remote(sent.at[0], final.at[0], final_send.at[0], final_recv.at[0], at(zx, yy, core, xx * 4 + zy))
    partner = jnp.where(zy != yy, jnp.where(yy < zy, core, 1 - core), 1 - core)
    to_turned = remote(sent.at[1], final.at[1], final_send.at[1], final_recv.at[1], at(xx, zy, partner, zx * 4 + yy))

    @pl.when(same_x)
    def _():
        final[0] = value

    @pl.when(jnp.logical_not(same_x))
    def _():
        sent[0] = value
        to_direct.start()

    turned[...] = flip_rows(value)
    flipped = jnp.concatenate(
        [
            jnp.concatenate([turned[pl.ds(16 * i + s, 4, stride=4), :] for i in range(6)], axis=1)
            for s in range(4)
        ],
        axis=0,
    )

    @pl.when(keep & jnp.logical_not(home))
    def _():
        final[1] = flipped

    @pl.when(jnp.logical_not(keep))
    def _():
        sent[1] = flipped
        to_turned.start()

    @pl.when(home)
    def _():
        for side in range(2):
            extra_merging(side).wait_recv()
            extra_chaining(side).wait_recv()
        final[1] = scaled(part[16] + (extra_merge[0] + extra_merge[1]) + (extra_chain[0] + extra_chain[1]))

    @pl.when(jnp.logical_not(same_x))
    def _():
        to_direct.wait_recv()

    @pl.when(jnp.logical_not(keep))
    def _():
        to_turned.wait_recv()

    first = jnp.where(
        zy != yy,
        jnp.where(yy < zy, core, 1 - core),
        jnp.where(zx <= xx, core, 1 - core),
    )
    one, two = final[0], final[1]
    low = jnp.where(first == 0, one, two)
    high = jnp.where(first == 0, two, one)
    for a in range(4):
        out[a] = jnp.concatenate([low[4 * a : 4 * a + 4, :WINDOW], high[4 * a : 4 * a + 4, :WINDOW]], axis=0)

    @pl.when(jnp.logical_not(same_x))
    def _():
        to_direct.wait_send()

    @pl.when(jnp.logical_not(keep))
    def _():
        to_turned.wait_send()

    for copy in gathers:
        copy.wait_send()
    for side in range(2):
        for i in range(4):
            merging(side, i, z).wait_send()
        for i in range(4 - side):
            chaining(side, i, z).wait_send()

    @pl.when(jnp.logical_not(home))
    def _():
        extra_merging(0).wait_send()


def body(x_tables, table, spectra, tilt_ranges):
    anywhere = pl.BlockSpec(memory_space=pl.ANY)
    f32, bf16 = jnp.float32, jnp.bfloat16
    dma = pltpu.SemaphoreType.DMA
    return pl.pallas_call(
        fused_kernel,
        out_shape=jax.ShapeDtypeStruct((4, 8, WINDOW), f32),
        in_specs=[anywhere] * 4,
        out_specs=pl.BlockSpec(memory_space=pltpu.VMEM),
        scratch_shapes=[
            pltpu.VMEM((4, 2, HALF, 256), bf16),
            pltpu.SMEM((2, 4), jnp.int32),
            pltpu.VMEM((LAGS, 8, 128), f32),
            pltpu.VMEM((2, 224, 256), bf16),
            pltpu.VMEM((4, HALF, 256), f32),
            pltpu.VMEM((128, 256), f32),
            pltpu.VMEM((HALF, 16, 128), f32),
            pltpu.VMEM((TILES, 16, 128), bf16),
            pltpu.VMEM((4, TILES, 16, 128), bf16),
            pltpu.VMEM((8, TILES, 16, 128), bf16),
            pltpu.VMEM((2, HALF, 288, 256), bf16),
            pltpu.VMEM((HALF, LAGS, 8, 128), f32),
            pltpu.VMEM((LAGS, LAGS, 8, 128), f32),
            pltpu.VMEM((88 * 8, 128), f32),
            pltpu.VMEM((17, 16, PADDED), f32),
            pltpu.VMEM((2, 4, 16, PADDED), f32),
            pltpu.VMEM((2, 4, 16, PADDED), f32),
            pltpu.VMEM((2, 16, PADDED), f32),
            pltpu.VMEM((2, 16, PADDED), f32),
            pltpu.VMEM((2, 16, PADDED), f32),
            pltpu.VMEM((2, 16, PADDED), f32),
            pltpu.VMEM((96, 128), f32),
            dma((4,)),
            dma((2, 4)),
            dma((2, 4)),
            dma((2, 4)),
            dma((2, 5)),
            dma((2, 4)),
            dma((2, 4)),
            dma((2, 4)),
            dma((2, 4)),
            dma((1,)),
            dma((2,)),
            dma((2,)),
            dma((2,)),
            dma((2,)),
        ],
        compiler_params=pltpu.CompilerParams(
            vmem_limit_bytes=60 * 1024 * 1024, collective_id=0, has_side_effects=True
        ),
    )(spectra, tilt_ranges.T, table, x_tables)


def solution(mesh):
    cols = mesh.shape["col"]
    inner = functools.partial(body, jnp.asarray(x_table(cols)), jnp.asarray(y_table()))
    return jax.shard_map(
        inner,
        mesh=mesh,
        in_specs=(P("row", None, None, "col"), P("row", None)),
        out_specs=P("row", "col", None),
        check_vma=False,
    )
```

```python
import functools
import math

import jax
import jax.numpy as jnp
import ml_dtypes
import numpy as np
from jax import lax
from jax.experimental import pallas as pl
from jax.experimental.pallas import tpu as pltpu
from jax.sharding import PartitionSpec as P

EDGE = 64
HALF = 33
REACH = 4
LAGS = 9
WINDOW = 729
PADDED = 768
TILES = HALF + 2
PIECE = 40
PARTS = ((0, 22), (22, HALF))
SPANS = ((0, 22), (22, TILES))
ROWS = 24
NT = (((1,), (1,)), ((), ()))


def split_np(x):
    high = x.astype(ml_dtypes.bfloat16)
    low = (x - high.astype(np.float64)).astype(ml_dtypes.bfloat16)
    return high, low


def y_table():
    freq = np.arange(EDGE)
    out = np.zeros((LAGS, 8, 128), np.float32)
    for i in range(LAGS):
        if i <= REACH:
            t = np.cos(2 * np.pi * freq * i / EDGE)
        else:
            t = np.sin(2 * np.pi * freq * (i - REACH) / EDGE)
        out[i, :, :EDGE] = t
        out[i, :4, EDGE:] = t
        out[i, 4:, EDGE:] = -t
    return out


def x_table(cols):
    out = np.zeros((cols, LAGS, ROWS, 2, 8, 4, 4), np.float64)
    for col in range(cols):
        for k in range(4):
            for lx in range(-REACH, REACH + 1):
                angle = 2 * np.pi * ((col * 4 + k) * lx % EDGE) / EDGE
                for r in range(ROWS // 4):
                    for s in range(4):
                        out[col, lx + REACH, r * 4 + s, 0, r, k, s] = math.cos(angle)
                        out[col, lx + REACH, r * 4 + s, 1, r, k, s] = -math.sin(angle)
    out = out.reshape(cols, LAGS * ROWS, 256)
    out = np.pad(out, ((0, 0), (0, 224 - LAGS * ROWS), (0, 0)))
    return np.stack(split_np(out), 1)


def z_coefs():
    weight = [1.0 if k in (0, 32) else 2.0 for k in range(HALF)]
    cos = [[weight[k] * math.cos(2 * math.pi * k * l / EDGE) for k in range(HALF)] for l in range(REACH + 1)]
    sin = [[weight[k] * math.sin(2 * math.pi * k * l / EDGE) for k in range(HALF)] for l in range(REACH + 1)]
    return cos, sin


def signed(freq_x):
    return jnp.where(freq_x < EDGE // 2, freq_x, freq_x - EDGE)


def observed(freq_z, freq_x, up, down):
    q = signed(freq_x)
    return 16 * freq_z <= jnp.where(q > 0, up, down) * jnp.abs(q)


def prepare_first(col, spectra, tilts, message, squares, pieces):
    lanes = lax.broadcasted_iota(jnp.int32, (HALF, 256), 1)
    freq_z = lax.broadcasted_iota(jnp.int32, (HALF, 256), 0)
    freq_x = col * 4 + lanes // EDGE
    weight = jnp.where((freq_z == 0) | (freq_z == EDGE // 2), 1.0, 2.0).astype(jnp.float32)
    for s in range(4):
        mask = observed(freq_z, freq_x, tilts[0, s], tilts[1, s])
        real = jnp.where(mask, spectra[s, 0].astype(jnp.float32), 0.0)
        imag = jnp.where(mask, spectra[s, 1].astype(jnp.float32), 0.0)
        squares[s] = (real * real + imag * imag) * weight
        for k in range(4):
            part = slice(k * EDGE, (k + 1) * EDGE)
            pieces[:, k * 4 + s, :] = jnp.concatenate([real[:, part], imag[:, part]], axis=1)
    first, last = PARTS[0]
    message[first:last] = pieces[first:last].astype(jnp.bfloat16)


def prepare_second(col, tilts, message, squares, power, pieces):
    first, last = PARTS[1]
    message[first:last] = pieces[first:last].astype(jnp.bfloat16)
    power[...] = jnp.zeros_like(power)
    row = lax.broadcasted_iota(jnp.int32, (16, 256), 0)
    lane = lax.broadcasted_iota(jnp.int32, (16, 256), 1)
    total = jnp.zeros((16, 128), jnp.float32)
    for s in range(4):
        for p in range(3):
            power[PIECE * p : PIECE * p + HALF, :] = squares[s]
        chosen = jnp.where((row // 4 == lane // EDGE) & (row % 4 == s), 1.0, 0.0)
        total = total + lax.dot_general(
            chosen, power[...], NT, precision=lax.Precision.HIGHEST, preferred_element_type=jnp.float32
        )
    lane = lax.broadcasted_iota(jnp.int32, (16, 128), 1)
    row = lax.broadcasted_iota(jnp.int32, (16, 128), 0)
    high = total.astype(jnp.bfloat16).astype(jnp.float32)
    rest = total - high
    mid = rest.astype(jnp.bfloat16).astype(jnp.float32)
    low = rest - mid
    third = lane // PIECE
    message[HALF] = jnp.where(third == 0, high, jnp.where(third == 1, mid, low)).astype(jnp.bfloat16)
    s = row % 4
    up, down = (
        jnp.where(s == 0, tilts[i, 0], jnp.where(s == 1, tilts[i, 1], jnp.where(s == 2, tilts[i, 2], tilts[i, 3])))
        for i in range(2)
    )
    at = lane - third * PIECE
    mask = observed(at, col * 4 + row // 4, up, down) & (at < HALF) & (third < 3)
    message[HALF + 1] = jnp.where(mask, 1.0, 0.0).astype(jnp.bfloat16)


def modulate(block, table, mod, part):
    def one(z, carry):
        base = block[z].astype(jnp.float32)
        turned = pltpu.roll(base, EDGE, 1)
        values = []
        for k in range(0, 4, 2):
            a, b = base[4 * k : 4 * k + 8], turned[4 * k : 4 * k + 8]
            for both in (
                jnp.where(first, a, pltpu.roll(b, 4, 0)),
                jnp.where(first, pltpu.roll(a, 4, 0), b),
            ):
                values += [both * table[i] for i in range(LAGS)]
        value = jnp.concatenate(values, axis=0)
        high = value.astype(jnp.bfloat16)
        mod[z, :, :128] = high
        mod[z, :, 128:] = (value - high.astype(jnp.float32)).astype(jnp.bfloat16)
        return carry

    first = lax.broadcasted_iota(jnp.int32, (8, 128), 0) < 4

    lax.fori_loop(*part, one, 0, unroll=11)


def window_tile(own, mod, blocks, depth, quads, middle, ready):
    lane_k = (lax.broadcasted_iota(jnp.int32, (8, 128), 1) // 4) % 4

    def diagonal(values):
        lane = jnp.concatenate([lane_k] * (values[0].shape[0] // 8), axis=0) if values[0].shape[0] > 8 else lane_k
        out = values[3]
        for k in (2, 1, 0):
            out = jnp.where(lane == k, values[k], out)
        return out

    def one(z, carry):
        tile = blocks(z)
        product = lax.dot_general(
            mod[z], jnp.concatenate([tile, tile], axis=1), NT, preferred_element_type=jnp.float32
        )
        depth[z] = diagonal([product[72 * k : 72 * k + 72] for k in range(4)]).reshape(LAGS, 8, 128)
        return carry

    for i, part in enumerate(PARTS):
        ready(i)
        lax.fori_loop(*part, one, 0, unroll=part[1] - part[0])

    middle()
    energies = []
    for own_tile, other in ((HALF, HALF + 1), (HALF + 1, HALF)):
        product = lax.dot_general(own[own_tile], blocks(other), NT, preferred_element_type=jnp.float32)
        picked = jnp.zeros((4, 128), jnp.float32)
        for k in range(4):
            picked = jnp.where(lane_k[:4] == k, product[4 * k : 4 * k + 4], picked)
        energies.append(jnp.concatenate([picked, jnp.zeros((4, 128), jnp.float32)], axis=0))

    cos, sin = z_coefs()

    def along_z(i, carry):
        value = [depth[z, i] for z in range(HALF)]
        even = [value[z] + value[32 - z] for z in range(16)] + [value[16]]
        odd = [value[z] - value[32 - z] for z in range(16)] + [value[16]]
        for lag in range(REACH + 1):
            source = even if lag % 2 == 0 else odd
            total = None
            for z in range(17):
                c = cos[lag][z]
                if z == 16 and lag % 2 == 1 or abs(c) < 1e-12:
                    continue
                term = source[z] * c
                total = term if total is None else total + term
            quads[lag, i] = total
        for lag in range(1, REACH + 1):
            source = odd if lag % 2 == 0 else even
            total = None
            for z in range(17):
                c = sin[lag][z]
                if z == 16 and lag % 2 == 0 or abs(c) < 1e-12:
                    continue
                term = source[z] * c
                total = term if total is None else total + term
            quads[REACH + lag, i] = total
        return carry

    lax.fori_loop(0, LAGS, along_z, 0, unroll=3)

    half = lax.broadcasted_iota(jnp.int32, (8, 128), 0) < 4

    def times_i(x):
        y = pltpu.roll(x, 4, 0)
        return jnp.where(half, -y, y)

    q = {}
    for ly in range(REACH + 1):
        for lz in range(REACH + 1):
            cc = quads[lz, ly]
            if ly == 0 and lz == 0:
                q[0, 0] = cc
            elif ly == 0:
                g = times_i(quads[REACH + lz, 0])
                q[0, lz], q[0, -lz] = cc + g, cc - g
            elif lz == 0:
                g = times_i(quads[0, REACH + ly])
                q[ly, 0], q[-ly, 0] = cc + g, cc - g
            else:
                ss = quads[REACH + lz, REACH + ly]
                sc = quads[lz, REACH + ly]
                cs = quads[REACH + lz, ly]
                p, m = cc - ss, cc + ss
                g, h = times_i(sc + cs), times_i(sc - cs)
                q[ly, lz], q[-ly, -lz] = p + g, p - g
                q[ly, -lz], q[-ly, lz] = m + h, m - h
    order = [q[ly, lz] for ly in range(-REACH, REACH + 1) for lz in range(-REACH, REACH + 1)] + energies
    order = order + [jnp.zeros((8, 128), jnp.float32)] * 5
    return order


def window_out(order_ref, xt, s):
    real = order_ref[pl.ds(s, 88, stride=8), :]
    imag = order_ref[pl.ds(4 + s, 88, stride=8), :]
    value = jnp.concatenate([real, imag], axis=1)
    high = value.astype(jnp.bfloat16)
    low = (value - high.astype(jnp.float32)).astype(jnp.bfloat16)
    x_high, x_low = xt[0], xt[1]
    dot = functools.partial(lax.dot_general, dimension_numbers=NT, preferred_element_type=jnp.float32)
    out = dot(x_high, high) + (dot(x_low, high) + dot(x_high, low))
    pieces = [out[ROWS * i : ROWS * i + ROWS, :81] for i in range(LAGS)]
    energy = out[ROWS * REACH : ROWS * REACH + ROWS, 81:83]
    fill = jnp.zeros((ROWS, PADDED - WINDOW - 2), jnp.float32)
    return jnp.concatenate(pieces + [energy, fill], axis=1)


def write_part(x, xx, yy, order, xt, part):
    first = lax.broadcasted_iota(jnp.int32, (8, PADDED), 0) < 4
    for pair in range(2):
        a, b = window_out(order, xt, 2 * pair), window_out(order, xt, 2 * pair + 1)
        blocks = []
        for i in range(0, ROWS, 8):
            upper, lower = a[i : i + 8], b[i : i + 8]
            blocks.append(jnp.where(first, upper, pltpu.roll(lower, 4, 0)))
            blocks.append(jnp.where(first, pltpu.roll(upper, 4, 0), lower))
        for y in range(4):
            swap = (yy == y) & (x < xx)
            part[x * 4 + y, 8 * pair : 8 * pair + 8, :] = jnp.where(swap, blocks[4], blocks[y])

        @pl.when(x == xx)
        def _():
            part[16, 8 * pair : 8 * pair + 8, :] = blocks[4]


def flip_rows(rows):
    moved = pltpu.roll(rows, PADDED - WINDOW, 1)
    stacked = jnp.concatenate([moved[:, 128 * (5 - i) : 128 * (6 - i)] for i in range(6)], axis=0)
    row = lax.broadcasted_iota(jnp.int32, (128, 128), 0)
    lane = lax.broadcasted_iota(jnp.int32, (128, 128), 1)
    swap = jnp.where(row + lane == 127, 1.0, 0.0).astype(jnp.bfloat16)
    out = None
    for _ in range(3):
        high = stacked.astype(jnp.bfloat16)
        stacked = stacked - high.astype(jnp.float32)
        part = jnp.dot(high, swap, preferred_element_type=jnp.float32)
        out = part if out is None else out + part
    return out


def fused_kernel(
    spectra_any, tilts_any, table_any, tables_any, out,
    spectra, tilts, table, xt, squares, power, pieces, own, mods, lanes, mod, depth, quads, order,
    part, merge, chain, extra_merge, extra_chain, sent, final, turned,
    local_sem, x_send, x_recv, y_send, y_recv, merge_send, merge_recv, chain_send, chain_recv,
    extra_send, extra_merge_recv, extra_chain_recv, final_send, final_recv,
):
    row = lax.axis_index("row")
    z = lax.axis_index("col")
    xx, yy, core = row // 8, (row // 2) % 4, row % 2
    zx, zy = z // 4, z % 4
    chip = xx * 4 + yy

    def at(x, y, c, depth_z):
        return {"row": (x * 4 + y) * 2 + c, "col": depth_z}

    def along(offset):
        return at(xx, yy, core, lax.rem(z + offset, 16))

    locals_ = [
        pltpu.make_async_copy(spectra_any, spectra, local_sem.at[0]),
        pltpu.make_async_copy(tilts_any, tilts, local_sem.at[1]),
        pltpu.make_async_copy(table_any, table, local_sem.at[2]),
        pltpu.make_async_copy(tables_any.at[z], xt, local_sem.at[3]),
    ]
    for copy in locals_:
        copy.start()

    barrier = pltpu.get_barrier_semaphore()

    def greet(target):
        pl.semaphore_signal(barrier, inc=1, device_id=target, device_id_type=pl.DeviceIdType.MESH)

    for i in range(1, 4):
        greet(at(lax.rem(xx + i, 4), yy, core, z))
        greet(at(xx, lax.rem(yy + i, 4), 0, z))
        greet(at(xx, lax.rem(yy + i, 4), 1, z))
    greet(at(xx, yy, 1 - core, z))
    for offset in (1, 15, 2, 14):
        greet(along(offset))

    @pl.when(zx != xx)
    def _():
        greet(at(zx, yy, core, xx * 4 + zy))

    @pl.when(zy != yy)
    def _():
        greet(at(xx, zy, 0, zx * 4 + yy))
        greet(at(xx, zy, 1, zx * 4 + yy))

    locals_[0].wait()
    locals_[1].wait()
    prepare_first(z, spectra, tilts, own, squares, pieces)
    count = 14 + jnp.where(zx != xx, 1, 0) + jnp.where(zy != yy, 2, 0)
    pl.semaphore_wait(barrier, count)

    def remote(src, dst, send, recv, target):
        return pltpu.make_async_remote_copy(
            src_ref=src, dst_ref=dst, send_sem=send, recv_sem=recv,
            device_id=target, device_id_type=pl.DeviceIdType.MESH,
        )

    gathers = []
    for i, span in enumerate(SPANS):
        if i == 1:
            prepare_second(z, tilts, own, squares, power, pieces)
        span = slice(*span)
        ready_now = []
        for n in (2, 1, 3):
            y = lax.rem(yy + n, 4)
            there = jnp.where(y < yy, core, 1 - core)
            ready_now.append(
                remote(own.at[span], lanes.at[yy, span], y_send.at[i, n], y_recv.at[i, yy], at(xx, y, there, z))
            )
        ready_now.append(
            remote(own.at[span], lanes.at[4, span], y_send.at[i, 0], y_recv.at[i, 4], at(xx, yy, 1 - core, z))
        )
        for n in (1, 3, 2):
            x = lax.rem(xx + n, 4)
            ready_now.append(
                remote(own.at[span], mods.at[xx, span], x_send.at[i, n], x_recv.at[i, xx], at(x, yy, core, z))
            )
        for copy in ready_now:
            copy.start()
        gathers += ready_now

    lanes[yy] = own[...]
    mods[xx] = own[...]
    lanes[5:8] = jnp.zeros((3, TILES, 16, 128), jnp.bfloat16)
    locals_[2].wait()
    modulate(own, table, mod.at[0], (0, HALF))
    locals_[3].wait()

    def wait_lane(i, slot):
        span = slice(*SPANS[i])
        remote(
            own.at[span], lanes.at[slot, span], y_send.at[i, 0], y_recv.at[i, slot], at(xx, yy, 1 - core, z)
        ).wait_recv()

    near_hop, far_hop = (1, 15), (2, 14)

    def merging(side, i, chunk):
        return remote(
            part.at[chunk], merge.at[side, i], merge_send.at[side, i], merge_recv.at[side, i], along(near_hop[side])
        )

    def chaining(side, i, chunk):
        return remote(
            part.at[chunk], chain.at[side, i], chain_send.at[side, i], chain_recv.at[side, i], along(far_hop[side])
        )

    def extra_merging(side):
        return remote(
            part.at[16], extra_merge.at[side], extra_send.at[0], extra_merge_recv.at[side], along(near_hop[side])
        )

    def extra_chaining(side):
        return remote(
            part.at[16], extra_chain.at[side], extra_send.at[0], extra_chain_recv.at[side], along(far_hop[side])
        )

    def spread(x):
        for k in range(4):
            chunk = x * 4 + k
            ahead = lax.rem(chunk + 16 - z, 16)
            odd = lax.rem(ahead, 2) == 1
            for side, here, gap in ((0, odd & (ahead < 8), ahead), (1, odd & (ahead > 8), 16 - ahead)):
                @pl.when(here)
                def _():
                    merging(side, gap // 2, chunk).start()

                    @pl.when(chunk == chip)
                    def _():
                        extra_merging(side).start()

    def step(side, gap):
        longest = 8 - 2 * side
        chunk = lax.rem(z + (gap, 16 - gap)[side], 16)
        order_at = (longest - gap) // 2
        merged, chained = gap < 8, gap < longest
        if merged:
            merging(side, gap // 2, chunk).wait_recv()
            part[chunk] = part[chunk] + merge[side, gap // 2]
        if chained:
            chaining(side, order_at - 1, chunk).wait_recv()
            part[chunk] = part[chunk] + chain[side, order_at - 1]
        chaining(side, order_at, chunk).start()

        @pl.when(chunk == chip)
        def _():
            if merged:
                extra_merging(side).wait_recv()
                part[16] = part[16] + extra_merge[side]
            if chained:
                extra_chaining(side).wait_recv()
                part[16] = part[16] + extra_chain[side]
            extra_chaining(side).start()

    second = jnp.where(zy < 2, 1, 3)

    def task(q, carry):
        turn = jnp.where(q == 0, 2, jnp.where(q == 1, second, jnp.where(q == 2, 4 - second, 0)))
        x = lax.rem(zx + turn, 4)

        def ready(i):
            @pl.when(x != xx)
            def _():
                span = slice(*SPANS[i])
                remote(
                    own.at[span], mods.at[x, span], x_send.at[i, 0], x_recv.at[i, x], at(xx, yy, 1 - core, z)
                ).wait_recv()
                modulate(mods.at[x], table, mod.at[1], PARTS[i])

            @pl.when(q == 0)
            def _():
                for n in range(1, 4):
                    wait_lane(i, lax.rem(yy + n, 4))
                wait_lane(i, 4)

        def middle():
            for at_q, gap in ((2, 6), (3, 4)):
                @pl.when(q == at_q)
                def _():
                    step(0, gap)
                    step(1, gap)

        def blocks(k):
            return lanes[:, k].reshape(128, 128)

        rows = window_tile(mods.at[x], mod.at[jnp.where(x == xx, 0, 1)], blocks, depth, quads, middle, ready)
        order[...] = jnp.concatenate(rows, axis=0)
        write_part(x, xx, yy, order, xt, part)

        spread(x)

        @pl.when(q == 0)
        def _():
            step(0, 8)

        return carry

    lax.fori_loop(0, 4, task, 0)
    step(0, 2)
    step(1, 2)
    for side in range(2):
        merging(side, 0, z).wait_recv()
        chaining(side, 3 - side, z).wait_recv()

    def scaled(total):
        return total / jnp.sqrt(total[:, WINDOW : WINDOW + 1] * total[:, WINDOW + 1 : WINDOW + 2])

    value = scaled(part[z] + (merge[0, 0] + merge[1, 0]) + (chain[0, 3] + chain[1, 2]))
    same_x = zx == xx
    home = z == chip
    keep = (zy == yy) & (zx >= xx)
    to_direct = remote(sent.at[0], final.at[0], final_send.at[0], final_recv.at[0], at(zx, yy, core, xx * 4 + zy))
    partner = jnp.where(zy != yy, jnp.where(yy < zy, core, 1 - core), 1 - core)
    to_turned = remote(sent.at[1], final.at[1], final_send.at[1], final_recv.at[1], at(xx, zy, partner, zx * 4 + yy))

    @pl.when(same_x)
    def _():
        final[0] = value

    @pl.when(jnp.logical_not(same_x))
    def _():
        sent[0] = value
        to_direct.start()

    turned[...] = flip_rows(value)
    flipped = jnp.concatenate(
        [
            jnp.concatenate([turned[pl.ds(16 * i + s, 4, stride=4), :] for i in range(6)], axis=1)
            for s in range(4)
        ],
        axis=0,
    )

    @pl.when(keep & jnp.logical_not(home))
    def _():
        final[1] = flipped

    @pl.when(jnp.logical_not(keep))
    def _():
        sent[1] = flipped
        to_turned.start()

    @pl.when(home)
    def _():
        for side in range(2):
            extra_merging(side).wait_recv()
            extra_chaining(side).wait_recv()
        final[1] = scaled(part[16] + (extra_merge[0] + extra_merge[1]) + (extra_chain[0] + extra_chain[1]))

    @pl.when(jnp.logical_not(same_x))
    def _():
        to_direct.wait_recv()

    @pl.when(jnp.logical_not(keep))
    def _():
        to_turned.wait_recv()

    first = jnp.where(
        zy != yy,
        jnp.where(yy < zy, core, 1 - core),
        jnp.where(zx <= xx, core, 1 - core),
    )
    one, two = final[0], final[1]
    low = jnp.where(first == 0, one, two)
    high = jnp.where(first == 0, two, one)
    for a in range(4):
        out[a] = jnp.concatenate([low[4 * a : 4 * a + 4, :WINDOW], high[4 * a : 4 * a + 4, :WINDOW]], axis=0)

    @pl.when(jnp.logical_not(same_x))
    def _():
        to_direct.wait_send()

    @pl.when(jnp.logical_not(keep))
    def _():
        to_turned.wait_send()

    for copy in gathers:
        copy.wait_send()
    for side in range(2):
        for i in range(4):
            merging(side, i, z).wait_send()
        for i in range(4 - side):
            chaining(side, i, z).wait_send()

    @pl.when(jnp.logical_not(home))
    def _():
        extra_merging(0).wait_send()


def body(x_tables, table, spectra, tilt_ranges):
    anywhere = pl.BlockSpec(memory_space=pl.ANY)
    f32, bf16 = jnp.float32, jnp.bfloat16
    dma = pltpu.SemaphoreType.DMA
    return pl.pallas_call(
        fused_kernel,
        out_shape=jax.ShapeDtypeStruct((4, 8, WINDOW), f32),
        in_specs=[anywhere] * 4,
        out_specs=pl.BlockSpec(memory_space=pltpu.VMEM),
        scratch_shapes=[
            pltpu.VMEM((4, 2, HALF, 256), bf16),
            pltpu.SMEM((2, 4), jnp.int32),
            pltpu.VMEM((LAGS, 8, 128), f32),
            pltpu.VMEM((2, 224, 256), bf16),
            pltpu.VMEM((4, HALF, 256), f32),
            pltpu.VMEM((128, 256), f32),
            pltpu.VMEM((HALF, 16, 128), f32),
            pltpu.VMEM((TILES, 16, 128), bf16),
            pltpu.VMEM((4, TILES, 16, 128), bf16),
            pltpu.VMEM((8, TILES, 16, 128), bf16),
            pltpu.VMEM((2, HALF, 288, 256), bf16),
            pltpu.VMEM((HALF, LAGS, 8, 128), f32),
            pltpu.VMEM((LAGS, LAGS, 8, 128), f32),
            pltpu.VMEM((88 * 8, 128), f32),
            pltpu.VMEM((17, 16, PADDED), f32),
            pltpu.VMEM((2, 4, 16, PADDED), f32),
            pltpu.VMEM((2, 4, 16, PADDED), f32),
            pltpu.VMEM((2, 16, PADDED), f32),
            pltpu.VMEM((2, 16, PADDED), f32),
            pltpu.VMEM((2, 16, PADDED), f32),
            pltpu.VMEM((2, 16, PADDED), f32),
            pltpu.VMEM((96, 128), f32),
            dma((4,)),
            dma((2, 4)),
            dma((2, 4)),
            dma((2, 4)),
            dma((2, 5)),
            dma((2, 4)),
            dma((2, 4)),
            dma((2, 4)),
            dma((2, 4)),
            dma((1,)),
            dma((2,)),
            dma((2,)),
            dma((2,)),
            dma((2,)),
        ],
        compiler_params=pltpu.CompilerParams(
            vmem_limit_bytes=60 * 1024 * 1024, collective_id=0, has_side_effects=True
        ),
    )(spectra, tilt_ranges.T, table, x_tables)


def solution(mesh):
    cols = mesh.shape["col"]
    inner = functools.partial(body, jnp.asarray(x_table(cols)), jnp.asarray(y_table()))
    return jax.shard_map(
        inner,
        mesh=mesh,
        in_specs=(P("row", None, None, "col"), P("row", None)),
        out_specs=P("row", "col", None),
        check_vma=False,
    )
```
